32 devices in a mesh: groups: 2 (over x), space: 4 (over y, core), frame: 4 (over z).
Axes of the slice: x: 2, y: 2, z: 4, core: 2. Of those that a mesh axis runs over, the one named last changes fastest.
Arguments:
- tokens: bfloat16 [4, 64, 128, 512], P('frame', ('groups', 'space')), parts along dimension 1, may hold values from -6 to 6
- src_brick: int32 [3, 64], P(None, 'groups'), parts along dimension 1, may hold values from 0 to 31, as said below
- merge_num: int32 [3, 64], P(None, 'groups'), parts along dimension 1, may hold values from 1 to 4
- gain_attn: float32 [512], replicated, may hold values from 0.1 to 1.9
- w_query: bfloat16 [512, 512], replicated, may hold values from -4 to 4
- w_key: bfloat16 [512, 512], replicated, may hold values from -4 to 4
- w_value: bfloat16 [512, 512], replicated, may hold values from -0.25 to 0.25
- w_out: bfloat16 [512, 512], replicated, may hold values from -0.25 to 0.25
- gain_mlp: float32 [512], replicated, may hold values from 0.1 to 1.9
- w_in: bfloat16 [512, 2048], replicated, may hold values from -0.25 to 0.25
- w_back: bfloat16 [2048, 512], replicated, may hold values from -0.125 to 0.125
Outputs:
- output: bfloat16 [4, 64, 128, 512], P('frame', ('groups', 'space')), parts along dimension 1
The draws below stay inside these ranges and needn't reach their ends.
There are 2 independent parts, one for each index of `groups`. The reference program is written for one: setup_inputs(seed, part) draws one part's arguments, and reference() takes and returns one part's arrays. A program takes and returns all parts, laid end to end along the dimension named above; an argument that names none is the same for every part. Nothing has to cross between parts.
Inputs may be any that keep to these rules, and one draw needn't show every extreme that they name: `src_brick`: group the bricks in aligned groups of 8. Over all frames, at most 7 entries pair a target brick of one group with a source brick of one group, and for every target group some source group is paired exactly 7 times.
All inputs are finite; a program needn't handle non-finite values.
Results may differ from the reference program's by a relative error of at most 0.0069.
Values may be sent and summed in bfloat16 or wider, within the bound.
No kernel may reach another device: no remote copies, remote signals or barrier semaphores. Data moves between devices by JAX's collectives and lax.ppermute only.
A program may use at most 64 MiB of HBM per device.

```python
import jax
import jax.numpy as jnp
from jax import lax

D = 512
HD = 64
FF = 2048
BT = 128
BR_DEV = 8
FRAMES = 4
BRICKS = 32
CAP = 7


def draw_src_brick(key, part):
    groups_all = BRICKS // BR_DEV
    request_total = (FRAMES - 1) * BR_DEV
    slot_total = groups_all * CAP

    def draw_row(requester):
        row_key = jax.random.fold_in(key, requester)
        key_hot, key_mix, key_order, key_pick = jax.random.split(row_key, 4)
        hot_owner = (requester + jax.random.randint(key_hot, (), -1, 2)) % groups_all
        owner_of = jnp.arange(slot_total) // CAP
        shuffle = jax.random.permutation(key_mix, slot_total)
        scores = jnp.where(owner_of == hot_owner, jnp.arange(slot_total), slot_total + shuffle)
        ordering = jnp.argsort(scores)
        chosen = owner_of[ordering[:request_total]]
        chosen = chosen[jax.random.permutation(key_order, request_total)]
        local_pick = jax.random.randint(key_pick, (request_total,), 0, BR_DEV)
        return (chosen * BR_DEV + local_pick).reshape(FRAMES - 1, BR_DEV)
    src_table = jax.vmap(draw_row)(jnp.arange(groups_all))
    return jnp.transpose(src_table, (1, 0, 2)).reshape(FRAMES - 1, BRICKS).astype(jnp.int32)


def projection(key, salt):
    noise_draw = jax.random.normal(jax.random.fold_in(key, salt), (D, D), jnp.float32)
    matrix_out = noise_draw * D ** (-0.5)
    return matrix_out.astype(jnp.bfloat16)


def draw_w_query(key, part):
    return projection(key, 21)


def draw_w_key(key, part):
    return projection(key, 22)


def place_ends(values, rng, least, high):
    dims = values.shape
    spot = [jax.random.randint(jax.random.fold_in(rng, axis), (), 0, dims[axis]) for axis in range(len(dims))]
    values = values.at[tuple(spot)].set(least)
    longest = dims.index(max(dims))
    spot[longest] = (spot[longest] + 1) % dims[longest]
    return values.at[tuple(spot)].set(high)


def block_levels(own_key, dims, shards, smallest, top_value):
    factor_of = 1.0
    for dim, parts in shards:
        steps = jax.random.uniform(jax.random.fold_in(jax.random.fold_in(own_key, 6), dim), (parts,), jnp.float32, smallest / len(shards), top_value / len(shards))
        factor_of = factor_of * jnp.repeat(jnp.exp(steps), dims[dim] // parts).reshape((-1,) + (1,) * (len(dims) - 1 - dim))
    return factor_of


def centred(own_key, shape, deviation, bound, shards=(), kind=jnp.bfloat16):
    drawn = jax.random.normal(own_key, shape, jnp.float32) * deviation
    if len(shards) > 0:
        drawn = block_levels(own_key, shape, shards, -0.22, 0.18) * drawn
    return jnp.clip(drawn, min=-bound, max=bound).astype(kind)


def setup_inputs(seed: int = 0, part: int = 0) -> dict:
    keys = jax.random.split(jax.random.key(seed), 12)
    part_splits = jax.random.split(jax.random.fold_in(keys[11], part), 12)
    return {
        "tokens": centred(part_splits[0], (FRAMES, BRICKS, BT, D), 1.0, 6.0, ((0, 4), (1, 4))),
        "src_brick": draw_src_brick(jax.random.fold_in(jax.random.fold_in(keys[11], part), 71), part),
        "merge_num": place_ends(jax.random.randint(part_splits[2], (FRAMES - 1, BRICKS), 1, 5), jax.random.fold_in(part_splits[2], 1), 1, 4).astype(jnp.int32),
        "gain_attn": jnp.clip(1.0 + 0.18 * jax.random.normal(keys[3], (D,), jnp.float32), 0.1, 1.9),
        "w_query": draw_w_query(jax.random.fold_in(keys[11], 71), part),
        "w_key": draw_w_key(jax.random.fold_in(keys[11], 71), part),
        "w_value": centred(keys[6], (D, D), D ** -0.5, 0.25),
        "w_out": centred(keys[7], (D, D), D ** -0.5, 0.25),
        "gain_mlp": jnp.clip(1.0 + 0.18 * jax.random.normal(keys[8], (D,), jnp.float32), 0.1, 1.9),
        "w_in": centred(keys[9], (D, FF), D ** -0.5, 0.25),
        "w_back": centred(keys[10], (FF, D), FF ** -0.5, 0.125),
    }


def rms_norm(values_in, gain):
    as_float = values_in.astype(jnp.float32)
    mean_sq = lax.optimization_barrier(jnp.mean(as_float * as_float, axis=-1, keepdims=True))
    return (as_float * lax.rsqrt(mean_sq + 1e-06) * gain.astype(jnp.float32)).astype(jnp.bfloat16)

def temporal_block(merged, gain_attn, w_query, w_key, w_value, w_out, gain_mlp, w_in, w_back):
    frames_all, rows_all = (merged.shape[0], merged.shape[1])
    heads = D // HD
    normed = rms_norm(merged, gain_attn)
    queries = jnp.dot(normed, w_query, preferred_element_type=jnp.float32).astype(jnp.bfloat16)
    keys_proj = jnp.dot(normed, w_key, preferred_element_type=jnp.float32).astype(jnp.bfloat16)
    values_proj = jnp.dot(normed, w_value, preferred_element_type=jnp.float32).astype(jnp.bfloat16)
    query_heads = queries.reshape(frames_all, rows_all, heads, HD).astype(jnp.float32)
    key_heads = keys_proj.reshape(frames_all, rows_all, heads, HD).astype(jnp.float32)
    value_heads = values_proj.reshape(frames_all, rows_all, heads, HD).astype(jnp.float32)
    scores = jnp.einsum('fmhd,gmhd->fghm', query_heads, key_heads) * (1.0 / HD ** 0.5)
    later = jnp.arange(frames_all)[:, None] >= jnp.arange(frames_all)[None, :]
    scores = jnp.where(later[:, :, None, None], scores, -1e+30)
    row_max = lax.optimization_barrier(jnp.max(scores, axis=1, keepdims=True))
    weights_exp = jnp.exp(scores - row_max)
    probs = (weights_exp / lax.optimization_barrier(jnp.sum(weights_exp, axis=1, keepdims=True))).astype(jnp.bfloat16)
    context = jnp.einsum('fghm,gmhd->fmhd', probs.astype(jnp.float32), value_heads)
    context = context.astype(jnp.bfloat16).reshape(frames_all, rows_all, D)
    mid = (merged.astype(jnp.float32) + jnp.dot(context, w_out, preferred_element_type=jnp.float32)).astype(jnp.bfloat16)
    normed2 = rms_norm(mid, gain_mlp)
    hidden = jax.nn.gelu(jnp.dot(normed2, w_in, preferred_element_type=jnp.float32)).astype(jnp.bfloat16)
    return (mid.astype(jnp.float32) + jnp.dot(hidden, w_back, preferred_element_type=jnp.float32)).astype(jnp.bfloat16)

def reference(tokens, src_brick, merge_num, gain_attn, w_query, w_key, w_value, w_out, gain_mlp, w_in, w_back):
    previous = tokens[:-1]
    moved = jax.vmap(lambda frame_rows, picks: jnp.take(frame_rows, picks, axis=0))(previous, src_brick)
    weight = merge_num.astype(jnp.float32) * 0.25
    merged_rest = (tokens[1:].astype(jnp.float32) + weight[:, :, None, None] * moved.astype(jnp.float32)).astype(jnp.bfloat16)
    merged = jnp.concatenate([tokens[:1], merged_rest], axis=0)
    by_brick = jnp.transpose(merged, (1, 0, 2, 3))

    def one_brick(brick_rows):
        return temporal_block(brick_rows, gain_attn, w_query, w_key, w_value, w_out, gain_mlp, w_in, w_back)
    result = lax.map(one_brick, by_brick)
    return jnp.transpose(result, (1, 0, 2, 3))
```

```python
import functools

import jax
import jax.numpy as jnp
from jax import lax
from jax.experimental import pallas as pl
from jax.experimental.pallas import tpu as pltpu
from jax.sharding import PartitionSpec as P

HD = 64
ROW_TILE = 16
BLOCK_FF = 512

VMEM = pltpu.VMEM
SMEM = pltpu.SMEM


def spec(space):
    return pl.BlockSpec(memory_space=space)


def exchange(values, axis, step):
    size = lax.axis_size(axis)
    return lax.ppermute(values, axis, [(i, i ^ step) for i in range(size)])


def table_kernel(cap, bricks, spaces, ids, src, send_tab, req_tab, count):
    requests = src.shape[0] * bricks
    me = ids[0]
    for owner in range(spaces):
        count[owner] = 0

    def one_request(q, carry):
        source = src[lax.div(q, bricks), me * bricks + lax.rem(q, bricks)]
        owner = lax.div(source, bricks)
        rank = count[owner]
        req_tab[q] = (owner ^ me) * cap + rank
        count[owner] = rank + 1
        return carry

    lax.fori_loop(0, requests, one_request, 0)

    for j in range(spaces):
        target = me ^ j

        def one_send(q, filled, target=target, j=j):
            frame = lax.div(q, bricks)
            source = src[frame, target * bricks + lax.rem(q, bricks)]
            owner = lax.div(source, bricks)
            send_tab[j * cap + filled] = frame * bricks + lax.rem(source, bricks)
            return filled + (owner == me).astype(jnp.int32)

        lax.fori_loop(0, requests, one_send, 0)


def plan_tables(ids, src_brick, cap, bricks, spaces):
    requests = src_brick.shape[0] * bricks
    return pl.pallas_call(
        functools.partial(table_kernel, cap, bricks, spaces),
        out_shape=(
            jax.ShapeDtypeStruct((spaces * cap + 1,), jnp.int32),
            jax.ShapeDtypeStruct((requests,), jnp.int32),
        ),
        in_specs=[spec(SMEM), spec(SMEM)],
        out_specs=(spec(SMEM), spec(SMEM)),
        scratch_shapes=[SMEM((spaces,), jnp.int32)],
        name="plan",
    )(ids, src_brick)


def select_kernel(frames, bricks, cap, spaces, *refs):
    ids, send_tab = refs[:2]
    parts = refs[2 : 2 + frames]
    stacked = refs[2 + frames]
    outs = refs[3 + frames :]
    mine = ids[1]
    for k in range(frames):
        stacked[pl.ds((mine ^ k) * bricks, bricks)] = parts[k][...]
    for j in list(range(1, spaces)) + [0]:
        for m in range(cap):
            outs[j][m] = stacked[send_tab[j * cap + m]]


def select(ids, send_tab, parts, cap, spaces):
    frames = len(parts)
    bricks, rows, width = parts[0].shape
    dtype = parts[0].dtype
    slots = jax.ShapeDtypeStruct((cap, rows, width), dtype)
    return pl.pallas_call(
        functools.partial(select_kernel, frames, bricks, cap, spaces),
        out_shape=(jax.ShapeDtypeStruct((frames * bricks, rows, width), dtype),)
        + (slots,) * spaces,
        in_specs=[spec(SMEM), spec(SMEM)] + [spec(VMEM)] * frames,
        out_specs=(spec(VMEM),) * (1 + spaces),
        compiler_params=pltpu.CompilerParams(vmem_limit_bytes=8 << 20),
        cost_estimate=pl.CostEstimate(flops=0, bytes_accessed=4 << 20, transcendentals=0),
        name="select",
    )(ids, send_tab, *parts)


def normalise(values, gain):
    wide = values.astype(jnp.float32)
    mean_sq = jnp.mean(wide * wide, axis=-1, keepdims=True)
    return (wide * lax.rsqrt(mean_sq + 1e-06) * gain).astype(jnp.bfloat16)


def matmul(a, b):
    return jnp.dot(a, b, preferred_element_type=jnp.float32)


def block_kernel(frames, bricks, cap, spaces, heads, *refs):
    ids, req_tab, merge_num, stacked = refs[:4]
    pieces = refs[4 : 4 + spaces]
    gain_a, w_q, w_k, w_v, w_o, gain_m, w_in, w_back = refs[4 + spaces : 12 + spaces]
    outs = refs[12 + spaces : 12 + spaces + frames]
    slots, merged, hidden, result = refs[12 + spaces + frames :]
    rows, width = stacked.shape[1:]
    per_frame = bricks * rows
    for j in range(spaces):
        slots[j * cap : (j + 1) * cap] = pieces[j][...]
    for b in range(bricks):
        merged[b * rows : (b + 1) * rows] = stacked[b]
    base = ids[0] * bricks
    for f in range(1, frames):
        for b in range(bricks):
            q = (f - 1) * bricks + b
            weight = merge_num[f - 1, base + b].astype(jnp.float32) * 0.25
            piece = slots[req_tab[q]].astype(jnp.float32)
            at = f * per_frame + b * rows
            merged[at : at + rows] = (
                stacked[f * bricks + b].astype(jnp.float32) + weight * piece
            ).astype(jnp.bfloat16)
    normed = normalise(merged[...], gain_a[...])
    queries = matmul(normed, w_q[...]).astype(jnp.bfloat16)
    keys = matmul(normed, w_k[...]).astype(jnp.bfloat16)
    vals = matmul(normed, w_v[...]).astype(jnp.bfloat16)

    def frame_of(x, f):
        return x[f * per_frame : (f + 1) * per_frame]

    lanes = 128
    head_of = lax.broadcasted_iota(jnp.int32, (width, lanes), 0) // HD
    gather_heads = (head_of == lax.broadcasted_iota(jnp.int32, (width, lanes), 1)).astype(
        jnp.bfloat16
    )
    head_to = lax.broadcasted_iota(jnp.int32, (lanes, width), 1) // HD
    spread_heads = (head_to == lax.broadcasted_iota(jnp.int32, (lanes, width), 0)).astype(
        jnp.bfloat16
    )
    for f in range(frames):
        query = frame_of(queries, f).astype(jnp.float32)
        scores = []
        for g in range(f + 1):
            product = query * frame_of(keys, g).astype(jnp.float32)
            high = product.astype(jnp.bfloat16)
            low = (product - high.astype(jnp.float32)).astype(jnp.bfloat16)
            scores.append(
                (matmul(high, gather_heads) + matmul(low, gather_heads)) * (1.0 / HD**0.5)
            )
        top = functools.reduce(jnp.maximum, scores)
        exps = [jnp.exp(s - top) for s in scores]
        total = functools.reduce(jnp.add, exps)
        context = None
        for g in range(f + 1):
            prob = (exps[g] / total).astype(jnp.bfloat16)
            term = matmul(prob, spread_heads) * frame_of(vals, g).astype(jnp.float32)
            context = term if context is None else context + term
        hidden[f * per_frame : (f + 1) * per_frame] = context.astype(jnp.bfloat16)
    mid = (merged[...].astype(jnp.float32) + matmul(hidden[...], w_o[...])).astype(jnp.bfloat16)
    normed2 = normalise(mid, gain_m[...])
    total = mid.astype(jnp.float32)
    depth = w_in.shape[1]
    step = min(BLOCK_FF, depth)
    for at in range(0, depth, step):
        part = jax.nn.gelu(matmul(normed2, w_in[:, at : at + step])).astype(jnp.bfloat16)
        total = total + matmul(part, w_back[at : at + step])
    result[...] = total.astype(jnp.bfloat16).reshape(result.shape)
    mine = ids[1]
    for k in range(frames):
        outs[k][...] = result[pl.ds((mine ^ k) * bricks, bricks)]


def run_block(ids, req_tab, merge_num, stacked, pieces, weights, frames, cap):
    spaces = len(pieces)
    total, rows, width = stacked.shape
    bricks = total // frames
    dtype = stacked.dtype
    return pl.pallas_call(
        functools.partial(block_kernel, frames, bricks, cap, spaces, width // HD),
        out_shape=(jax.ShapeDtypeStruct((bricks, rows, width), dtype),) * frames,
        in_specs=[spec(SMEM)] * 3 + [spec(VMEM)] * (1 + spaces + len(weights)),
        out_specs=(spec(VMEM),) * frames,
        scratch_shapes=[
            VMEM((spaces * cap, rows, width), dtype),
            VMEM((total * rows, width), dtype),
            VMEM((total * rows, width), dtype),
            VMEM((total, rows, width), dtype),
        ],
        compiler_params=pltpu.CompilerParams(vmem_limit_bytes=32 << 20),
        cost_estimate=pl.CostEstimate(
            flops=6_400_000_000, bytes_accessed=8 << 20, transcendentals=1 << 20
        ),
        name="block",
    )(ids, req_tab, merge_num, stacked, *pieces, *weights)


def assemble_kernel(count, mine_at, *refs):
    ids = refs[0]
    parts = refs[1 : 1 + count]
    out, sems = refs[1 + count :]
    copies = [
        pltpu.make_async_copy(parts[i], out.at[:, mine_at(i, ids[1])], sems.at[i])
        for i in range(count)
    ]
    for copy in copies:
        copy.start()
    for copy in copies:
        copy.wait()


def assemble(ids, parts, frames):
    count = len(parts)
    bricks, rows, width = parts[0].shape

    def mine_at(i, mine):
        return i // frames * frames + (mine ^ (i % frames))

    return pl.pallas_call(
        functools.partial(assemble_kernel, count, mine_at),
        out_shape=jax.ShapeDtypeStruct((bricks, count, rows, width), parts[0].dtype),
        in_specs=[spec(SMEM)] + [spec(VMEM)] * count,
        out_specs=spec(pl.ANY),
        scratch_shapes=[pltpu.SemaphoreType.DMA((count,))],
        compiler_params=pltpu.CompilerParams(vmem_limit_bytes=4 << 20),
        name="assemble",
    )(ids, *parts)


def local(tokens, src_brick, merge_num, gain_attn, w_q, w_k, w_v, w_out, gain_mlp, w_in, w_back):
    frames = lax.axis_size("frame")
    spaces = lax.axis_size("space")
    _, bricks, tall, width = tokens.shape
    cap = max(2, (frames - 1) * bricks // spaces + 1)
    chunks = max(1, tall // frames // ROW_TILE)
    rows = tall // frames // chunks
    mine = lax.axis_index("frame")
    ids = jnp.stack([lax.axis_index("space"), mine]).astype(jnp.int32)
    cut = tokens.reshape(bricks, chunks * frames, rows, width)
    weights = (gain_attn[None], w_q, w_k, w_v, w_out, gain_mlp[None], w_in, w_back)
    send_tab, req_tab = plan_tables(ids, src_brick, cap, bricks, spaces)

    arrived = []
    for c in range(chunks):
        parts = [
            lax.dynamic_index_in_dim(cut, c * frames + (mine ^ k), 1, keepdims=False)
            for k in range(frames)
        ]
        if arrived:
            held = lax.optimization_barrier((tuple(parts), tuple(arrived[-1])))
            parts, arrived[-1] = list(held[0]), list(held[1])
        arrived.append(
            [parts[0]] + [exchange(parts[k], "frame", k) for k in range(1, frames)]
        )
    back = []
    for c in range(chunks):
        stacked, *slots = select(ids, send_tab, arrived[c], cap, spaces)
        pieces = [slots[0]] + [exchange(slots[j], "space", j) for j in range(1, spaces)]
        done = run_block(ids, req_tab, merge_num, stacked, pieces, weights, frames, cap)
        back += [done[0]] + [exchange(done[k], "frame", k) for k in range(1, frames)]
    out = assemble(ids, back, frames)
    return out.reshape(1, bricks, tall, width)


def solution(mesh):
    tokens = P("frame", ("groups", "space"), None, None)
    tables = P(None, "groups")
    in_specs = (tokens, tables, tables) + (P(),) * 8
    return jax.shard_map(local, mesh=mesh, in_specs=in_specs, out_specs=tokens, check_vma=False)
```

```python
import functools

import jax
import jax.numpy as jnp
from jax import lax
from jax.experimental import pallas as pl
from jax.experimental.pallas import tpu as pltpu
from jax.sharding import PartitionSpec as P

HD = 64
ROW_TILE = 16
BLOCK_FF = 512

VMEM = pltpu.VMEM
SMEM = pltpu.SMEM


def spec(space):
    return pl.BlockSpec(memory_space=space)


def exchange(values, axis, step):
    size = lax.axis_size(axis)
    return lax.ppermute(values, axis, [(i, i ^ step) for i in range(size)])


def pinned(values, space):
    return [pltpu.with_memory_space_constraint(v, space) for v in values]


class Layout:
    def __init__(self, frames, bricks, spaces, cap):
        self.frames, self.bricks, self.spaces, self.cap = frames, bricks, spaces, cap
        self.requests = (frames - 1) * bricks
        self.send = 2
        self.take = self.send + spaces * cap + 1
        self.weight = self.take + self.requests
        self.size = self.weight + self.requests


def prepare_kernel(lay, ids, src, merge_num, *refs):
    count = refs[-2]
    sems = refs[-1]
    half = (len(refs) - 3) // 2
    stored, table, loaded = refs[:half], refs[half], refs[half + 1 : -2]
    loads = [
        pltpu.make_async_copy(stored[i], loaded[i], sems.at[i]) for i in range(half)
    ]
    for load in loads:
        load.start()
    bricks, cap = lay.bricks, lay.cap
    me = ids[0]
    table[0] = me
    table[1] = ids[1]
    for owner in range(lay.spaces):
        count[owner] = 0

    def one_request(q, carry):
        frame, brick = lax.div(q, bricks), me * bricks + lax.rem(q, bricks)
        owner = lax.div(src[frame, brick], bricks)
        rank = count[owner]
        table[lay.take + q] = (owner ^ me) * cap + rank
        table[lay.weight + q] = merge_num[frame, brick]
        count[owner] = rank + 1
        return carry

    lax.fori_loop(0, lay.requests, one_request, 0)

    for j in range(lay.spaces):
        target = me ^ j

        def one_send(q, filled, target=target, j=j):
            frame = lax.div(q, bricks)
            source = src[frame, target * bricks + lax.rem(q, bricks)]
            owner = lax.div(source, bricks)
            table[lay.send + j * cap + filled] = frame * bricks + lax.rem(source, bricks)
            return filled + (owner == me).astype(jnp.int32)

        lax.fori_loop(0, lay.requests, one_send, 0)
    for load in loads:
        load.wait()


def prepare(lay, ids, src_brick, merge_num, weights):
    return pl.pallas_call(
        functools.partial(prepare_kernel, lay),
        out_shape=(pltpu.SMEM((lay.size,), jnp.int32),)
        + tuple(pltpu.VMEM(w.shape, w.dtype) for w in weights),
        in_specs=[spec(SMEM)] * 3 + [spec(pltpu.HBM)] * len(weights),
        out_specs=(spec(SMEM),) + (spec(VMEM),) * len(weights),
        scratch_shapes=[
            SMEM((lay.spaces,), jnp.int32),
            pltpu.SemaphoreType.DMA((len(weights),)),
        ],
        compiler_params=pltpu.CompilerParams(vmem_limit_bytes=1 << 20),
        name="prepare",
    )(ids, src_brick, merge_num, *pinned(weights, pltpu.HBM))


def select_kernel(lay, *refs):
    frames = lay.frames
    table = refs[0]
    parts = refs[1 : 1 + frames]
    stacked = refs[1 + frames]
    outs = refs[2 + frames :]
    mine = table[1]
    for k in range(frames):
        stacked[pl.ds((mine ^ k) * lay.bricks, lay.bricks)] = parts[k][...]
    for j in list(range(1, lay.spaces)) + [0]:
        for m in range(lay.cap):
            outs[j][m] = stacked[table[lay.send + j * lay.cap + m]]


def select(lay, table, parts):
    bricks, rows, width = parts[0].shape
    dtype = parts[0].dtype
    return pl.pallas_call(
        functools.partial(select_kernel, lay),
        out_shape=(jax.ShapeDtypeStruct((lay.frames * bricks, rows, width), dtype),)
        + (jax.ShapeDtypeStruct((lay.cap, rows, width), dtype),) * lay.spaces,
        in_specs=[spec(SMEM)] + [spec(VMEM)] * lay.frames,
        out_specs=(spec(VMEM),) * (1 + lay.spaces),
        compiler_params=pltpu.CompilerParams(vmem_limit_bytes=4 << 20),
        name="select",
    )(*pinned([table], SMEM), *parts)


def normalise(values, gain):
    wide = values.astype(jnp.float32)
    mean_sq = jnp.mean(wide * wide, axis=-1, keepdims=True)
    return (wide * lax.rsqrt(mean_sq + 1e-06) * gain).astype(jnp.bfloat16)


def matmul(a, b):
    return jnp.dot(a, b, preferred_element_type=jnp.float32)


def block_kernel(lay, *refs):
    frames, bricks, cap, spaces = lay.frames, lay.bricks, lay.cap, lay.spaces
    table, stacked = refs[:2]
    pieces = refs[2 : 2 + spaces]
    gain_a, gain_m, w_q, w_k, w_v, w_o, w_in, w_back = refs[2 + spaces : 10 + spaces]
    outs = refs[10 + spaces : 10 + spaces + frames]
    slots, merged, hidden, result = refs[10 + spaces + frames :]
    rows, width = stacked.shape[1:]
    per_frame = bricks * rows
    for j in range(spaces):
        slots[j * cap : (j + 1) * cap] = pieces[j][...]
    for b in range(bricks):
        merged[b * rows : (b + 1) * rows] = stacked[b]
    for f in range(1, frames):
        for b in range(bricks):
            q = (f - 1) * bricks + b
            weight = table[lay.weight + q].astype(jnp.float32) * 0.25
            piece = slots[table[lay.take + q]].astype(jnp.float32)
            at = f * per_frame + b * rows
            merged[at : at + rows] = (
                stacked[f * bricks + b].astype(jnp.float32) + weight * piece
            ).astype(jnp.bfloat16)
    normed = normalise(merged[...], gain_a[...])
    queries = matmul(normed, w_q[...]).astype(jnp.bfloat16)
    keys = matmul(normed, w_k[...]).astype(jnp.bfloat16)
    vals = matmul(normed, w_v[...]).astype(jnp.bfloat16)

    def frame_of(x, f):
        return x[f * per_frame : (f + 1) * per_frame]

    lanes = 128
    head_of = lax.broadcasted_iota(jnp.int32, (width, lanes), 0) // HD
    gather_heads = (head_of == lax.broadcasted_iota(jnp.int32, (width, lanes), 1)).astype(
        jnp.bfloat16
    )
    head_to = lax.broadcasted_iota(jnp.int32, (lanes, width), 1) // HD
    spread_heads = (head_to == lax.broadcasted_iota(jnp.int32, (lanes, width), 0)).astype(
        jnp.bfloat16
    )
    for f in range(frames):
        query = frame_of(queries, f).astype(jnp.float32)
        scores = []
        for g in range(f + 1):
            product = query * frame_of(keys, g).astype(jnp.float32)
            high = product.astype(jnp.bfloat16)
            low = (product - high.astype(jnp.float32)).astype(jnp.bfloat16)
            scores.append(
                (matmul(high, gather_heads) + matmul(low, gather_heads)) * (1.0 / HD**0.5)
            )
        top = functools.reduce(jnp.maximum, scores)
        exps = [jnp.exp(s - top) for s in scores]
        total = functools.reduce(jnp.add, exps)
        context = None
        for g in range(f + 1):
            prob = (exps[g] / total).astype(jnp.bfloat16)
            term = matmul(prob, spread_heads) * frame_of(vals, g).astype(jnp.float32)
            context = term if context is None else context + term
        hidden[f * per_frame : (f + 1) * per_frame] = context.astype(jnp.bfloat16)
    mid = (merged[...].astype(jnp.float32) + matmul(hidden[...], w_o[...])).astype(jnp.bfloat16)
    normed2 = normalise(mid, gain_m[...])
    total = mid.astype(jnp.float32)
    depth = w_in.shape[1]
    step = min(BLOCK_FF, depth)
    for at in range(0, depth, step):
        part = jax.nn.gelu(matmul(normed2, w_in[:, at : at + step])).astype(jnp.bfloat16)
        total = total + matmul(part, w_back[at : at + step])
    result[...] = total.astype(jnp.bfloat16).reshape(result.shape)
    mine = table[1]
    for k in range(frames):
        outs[k][...] = result[pl.ds((mine ^ k) * bricks, bricks)]


def run_block(lay, table, stacked, pieces, gains, weights):
    total, rows, width = stacked.shape
    dtype = stacked.dtype
    return pl.pallas_call(
        functools.partial(block_kernel, lay),
        out_shape=(jax.ShapeDtypeStruct((lay.bricks, rows, width), dtype),) * lay.frames,
        in_specs=[spec(SMEM)]
        + [spec(VMEM)] * (1 + lay.spaces + len(gains) + len(weights)),
        out_specs=(spec(VMEM),) * lay.frames,
        scratch_shapes=[
            VMEM((lay.spaces * lay.cap, rows, width), dtype),
            VMEM((total * rows, width), dtype),
            VMEM((total * rows, width), dtype),
            VMEM((total, rows, width), dtype),
        ],
        compiler_params=pltpu.CompilerParams(vmem_limit_bytes=20 << 20),
        name="block",
    )(*pinned([table], SMEM), stacked, *pieces, *gains, *pinned(weights, VMEM))


def assemble_kernel(count, mine_at, *refs):
    table = refs[0]
    parts = refs[1 : 1 + count]
    out, sems = refs[1 + count :]
    copies = [
        pltpu.make_async_copy(parts[i], out.at[:, mine_at(i, table[1])], sems.at[i])
        for i in range(count)
    ]
    for copy in copies:
        copy.start()
    for copy in copies:
        copy.wait()


def assemble(table, parts, frames):
    count = len(parts)
    bricks, rows, width = parts[0].shape

    def mine_at(i, mine):
        return i // frames * frames + (mine ^ (i % frames))

    return pl.pallas_call(
        functools.partial(assemble_kernel, count, mine_at),
        out_shape=jax.ShapeDtypeStruct((bricks, count, rows, width), parts[0].dtype),
        in_specs=[spec(SMEM)] + [spec(VMEM)] * count,
        out_specs=spec(pl.ANY),
        scratch_shapes=[pltpu.SemaphoreType.DMA((count,))],
        compiler_params=pltpu.CompilerParams(vmem_limit_bytes=4 << 20),
        name="assemble",
    )(*pinned([table], SMEM), *parts)


def local(tokens, src_brick, merge_num, gain_attn, w_q, w_k, w_v, w_out, gain_mlp, w_in, w_back):
    frames = lax.axis_size("frame")
    spaces = lax.axis_size("space")
    _, bricks, tall, width = tokens.shape
    cap = max(2, (frames - 1) * bricks // spaces + 1)
    chunks = max(1, tall // frames // ROW_TILE)
    rows = tall // frames // chunks
    mine = lax.axis_index("frame")
    ids = jnp.stack([lax.axis_index("space"), mine]).astype(jnp.int32)
    cut = tokens.reshape(bricks, chunks * frames, rows, width)
    lay = Layout(frames, bricks, spaces, cap)
    gains = (gain_attn[None], gain_mlp[None])
    weights = (w_q, w_k, w_v, w_out, w_in, w_back)

    def across(parts, axis):
        return [exchange(part, axis, k) for k, part in enumerate(parts, 1)]

    parts = [
        [
            lax.dynamic_index_in_dim(cut, c * frames + (mine ^ k), 1, keepdims=False)
            for k in range(frames)
        ]
        for c in range(chunks)
    ]
    (src_brick, merge_num), parts = lax.optimization_barrier(((src_brick, merge_num), parts))
    arrived = [across(parts[0][1:], "frame")]
    table, *weights = prepare(lay, ids, src_brick, merge_num, weights)
    for c in range(1, chunks):
        leaving, table, arrived[-1][0] = lax.optimization_barrier(
            (parts[c][1:], table, arrived[-1][0])
        )
        arrived.append(across(leaving, "frame"))
    back = []
    for c in range(chunks):
        stacked, *slots = select(lay, table, [parts[c][0]] + arrived[c])
        pieces = [slots[0]] + across(slots[1:], "space")
        done = run_block(lay, table, stacked, pieces, gains, weights)
        if c + 1 < chunks:
            arrived[c + 1], done = lax.optimization_barrier((arrived[c + 1], done))
        back += [done[0]] + across(done[1:], "frame")
    out = assemble(table, back, frames)
    return out.reshape(1, bricks, tall, width)


def solution(mesh):
    tokens = P("frame", ("groups", "space"), None, None)
    tables = P(None, "groups")
    in_specs = (tokens, tables, tables) + (P(),) * 8
    return jax.shard_map(local, mesh=mesh, in_specs=in_specs, out_specs=tokens, check_vma=False)
```

```python
import functools

import jax
import jax.numpy as jnp
from jax import lax
from jax.experimental import pallas as pl
from jax.experimental.pallas import tpu as pltpu
from jax.sharding import PartitionSpec as P

HD = 64
ROW_TILE = 16
BLOCK_FF = 512
TURNED = 3

VMEM = pltpu.VMEM
SMEM = pltpu.SMEM


def spec(space):
    return pl.BlockSpec(memory_space=space)


def exchange(values, axis, step):
    size = lax.axis_size(axis)
    return lax.ppermute(values, axis, [(i, i ^ step) for i in range(size)])


def pinned(values, space):
    return [pltpu.with_memory_space_constraint(v, space) for v in values]


class Layout:
    def __init__(self, frames, bricks, spaces, cap):
        self.frames, self.bricks, self.spaces, self.cap = frames, bricks, spaces, cap
        self.requests = (frames - 1) * bricks
        self.send = 2
        self.take = self.send + spaces * cap + 1
        self.weight = self.take + self.requests
        self.size = self.weight + self.requests


def prepare_kernel(lay, ids, src, merge_num, *refs):
    held, count, sems = refs[-3:]
    half = (len(refs) - 4) // 2
    stored, table, loaded = refs[:half], refs[half], refs[half + 1 : -3]
    loads = [
        pltpu.make_async_copy(
            stored[i], held.at[i] if i < TURNED else loaded[i], sems.at[i]
        )
        for i in range(half)
    ]
    for load in loads:
        load.start()
    bricks, cap = lay.bricks, lay.cap
    me = ids[0]
    table[0] = me
    table[1] = ids[1]
    for owner in range(lay.spaces):
        count[owner] = 0

    def one_request(q, carry):
        frame, brick = lax.div(q, bricks), me * bricks + lax.rem(q, bricks)
        owner = lax.div(src[frame, brick], bricks)
        rank = count[owner]
        table[lay.take + q] = (owner ^ me) * cap + rank
        table[lay.weight + q] = merge_num[frame, brick]
        count[owner] = rank + 1
        return carry

    lax.fori_loop(0, lay.requests, one_request, 0)

    for i in range(TURNED):
        loads[i].wait()
        loaded[i][...] = held[i].T

    for j in range(lay.spaces):
        target = me ^ j

        def one_send(q, filled, target=target, j=j):
            frame = lax.div(q, bricks)
            source = src[frame, target * bricks + lax.rem(q, bricks)]
            owner = lax.div(source, bricks)
            table[lay.send + j * cap + filled] = frame * bricks + lax.rem(source, bricks)
            return filled + (owner == me).astype(jnp.int32)

        lax.fori_loop(0, lay.requests, one_send, 0)
    for load in loads[TURNED:]:
        load.wait()


def prepare(lay, ids, src_brick, merge_num, weights):
    return pl.pallas_call(
        functools.partial(prepare_kernel, lay),
        out_shape=(pltpu.SMEM((lay.size,), jnp.int32),)
        + tuple(pltpu.VMEM(w.shape, w.dtype) for w in weights),
        in_specs=[spec(SMEM)] * 3 + [spec(pltpu.HBM)] * len(weights),
        out_specs=(spec(SMEM),) + (spec(VMEM),) * len(weights),
        scratch_shapes=[
            VMEM((TURNED,) + weights[0].shape, weights[0].dtype),
            SMEM((lay.spaces,), jnp.int32),
            pltpu.SemaphoreType.DMA((len(weights),)),
        ],
        compiler_params=pltpu.CompilerParams(vmem_limit_bytes=6 << 20),
        name="prepare",
    )(ids, src_brick, merge_num, *pinned(weights, pltpu.HBM))


def select_kernel(lay, *refs):
    frames = lay.frames
    table = refs[0]
    parts = refs[1 : 1 + frames]
    stacked = refs[1 + frames]
    outs = refs[2 + frames :]
    mine = table[1]
    for k in range(frames):
        stacked[pl.ds((mine ^ k) * lay.bricks, lay.bricks)] = parts[k][...]
    for j in list(range(1, lay.spaces)) + [0]:
        for m in range(lay.cap):
            outs[j][m] = stacked[table[lay.send + j * lay.cap + m]]


def select(lay, table, parts):
    bricks, rows, width = parts[0].shape
    dtype = parts[0].dtype
    return pl.pallas_call(
        functools.partial(select_kernel, lay),
        out_shape=(jax.ShapeDtypeStruct((lay.frames * bricks, rows, width), dtype),)
        + (jax.ShapeDtypeStruct((lay.cap, rows, width), dtype),) * lay.spaces,
        in_specs=[spec(SMEM)] + [spec(VMEM)] * lay.frames,
        out_specs=(spec(VMEM),) * (1 + lay.spaces),
        compiler_params=pltpu.CompilerParams(vmem_limit_bytes=4 << 20),
        cost_estimate=pl.CostEstimate(flops=1, bytes_accessed=0, transcendentals=0),
        name="select",
    )(*pinned([table], SMEM), *parts)


def normalise(values, gain):
    wide = values.astype(jnp.float32)
    mean_sq = jnp.mean(wide * wide, axis=-1, keepdims=True)
    return (wide * lax.rsqrt(mean_sq + 1e-06) * gain).astype(jnp.bfloat16)


def project_turned(turned, values):
    out = lax.dot_general(
        turned, values, (((1,), (1,)), ((), ())), preferred_element_type=jnp.float32
    )
    return out.astype(jnp.bfloat16)


def matmul(a, b):
    return jnp.dot(a, b, preferred_element_type=jnp.float32)


def block_kernel(lay, *refs):
    frames, bricks, cap, spaces = lay.frames, lay.bricks, lay.cap, lay.spaces
    table, stacked = refs[:2]
    pieces = refs[2 : 2 + spaces]
    gain_a, gain_m, w_q, w_k, w_v, w_o, w_in, w_back = refs[2 + spaces : 10 + spaces]
    outs = refs[10 + spaces : 10 + spaces + frames]
    slots, merged, hidden, result = refs[10 + spaces + frames :]
    rows, width = stacked.shape[1:]
    per_frame = bricks * rows
    for j in range(spaces):
        slots[j * cap : (j + 1) * cap] = pieces[j][...]
    for b in range(bricks):
        merged[b * rows : (b + 1) * rows] = stacked[b]
    for f in range(1, frames):
        for b in range(bricks):
            q = (f - 1) * bricks + b
            weight = table[lay.weight + q].astype(jnp.float32) * 0.25
            piece = slots[table[lay.take + q]].astype(jnp.float32)
            at = f * per_frame + b * rows
            merged[at : at + rows] = (
                stacked[f * bricks + b].astype(jnp.float32) + weight * piece
            ).astype(jnp.bfloat16)
    normed = normalise(merged[...], gain_a[...])
    queries = project_turned(w_q[...], normed)
    keys = project_turned(w_k[...], normed)
    vals = project_turned(w_v[...], normed)

    def heads_of(x, f):
        part = x[:, f * per_frame : (f + 1) * per_frame].astype(jnp.float32)
        return part.reshape(width // HD, HD, per_frame)

    for f in range(frames):
        query = heads_of(queries, f) * (1.0 / HD**0.5)
        scores = [
            jnp.sum(query * heads_of(keys, g), axis=1, keepdims=True) for g in range(f + 1)
        ]
        top = functools.reduce(jnp.maximum, scores)
        exps = [jnp.exp(s - top) for s in scores]
        total = functools.reduce(jnp.add, exps)
        context = None
        for g in range(f + 1):
            prob = (exps[g] / total).astype(jnp.bfloat16).astype(jnp.float32)
            term = prob * heads_of(vals, g)
            context = term if context is None else context + term
        context = context.reshape(width, per_frame).astype(jnp.bfloat16)
        hidden[f * per_frame : (f + 1) * per_frame] = context.T
    mid = (merged[...].astype(jnp.float32) + matmul(hidden[...], w_o[...])).astype(jnp.bfloat16)
    normed2 = normalise(mid, gain_m[...])
    total = mid.astype(jnp.float32)
    depth = w_in.shape[1]
    step = min(BLOCK_FF, depth)
    for at in range(0, depth, step):
        part = jax.nn.gelu(matmul(normed2, w_in[:, at : at + step])).astype(jnp.bfloat16)
        total = total + matmul(part, w_back[at : at + step])
    result[...] = total.astype(jnp.bfloat16).reshape(result.shape)
    mine = table[1]
    for k in range(frames):
        outs[k][...] = result[pl.ds((mine ^ k) * bricks, bricks)]


def run_block(lay, table, stacked, pieces, gains, weights):
    total, rows, width = stacked.shape
    dtype = stacked.dtype
    return pl.pallas_call(
        functools.partial(block_kernel, lay),
        out_shape=(jax.ShapeDtypeStruct((lay.bricks, rows, width), dtype),) * lay.frames,
        in_specs=[spec(SMEM)]
        + [spec(VMEM)] * (1 + lay.spaces + len(gains) + len(weights)),
        out_specs=(spec(VMEM),) * lay.frames,
        scratch_shapes=[
            VMEM((lay.spaces * lay.cap, rows, width), dtype),
            VMEM((total * rows, width), dtype),
            VMEM((total * rows, width), dtype),
            VMEM((total, rows, width), dtype),
        ],
        compiler_params=pltpu.CompilerParams(vmem_limit_bytes=20 << 20),
        cost_estimate=pl.CostEstimate(flops=10000000000, bytes_accessed=0, transcendentals=0),
        name="block",
    )(*pinned([table], SMEM), stacked, *pieces, *gains, *pinned(weights, VMEM))


def assemble_kernel(count, mine_at, *refs):
    table = refs[0]
    parts = refs[1 : 1 + count]
    out, sems = refs[1 + count :]
    copies = [
        pltpu.make_async_copy(parts[i], out.at[:, mine_at(i, table[1])], sems.at[i])
        for i in range(count)
    ]
    for copy in copies:
        copy.start()
    for copy in copies:
        copy.wait()


def assemble(table, parts, frames):
    count = len(parts)
    bricks, rows, width = parts[0].shape

    def mine_at(i, mine):
        return i // frames * frames + (mine ^ (i % frames))

    return pl.pallas_call(
        functools.partial(assemble_kernel, count, mine_at),
        out_shape=jax.ShapeDtypeStruct((bricks, count, rows, width), parts[0].dtype),
        in_specs=[spec(SMEM)] + [spec(VMEM)] * count,
        out_specs=spec(pl.ANY),
        scratch_shapes=[pltpu.SemaphoreType.DMA((count,))],
        compiler_params=pltpu.CompilerParams(vmem_limit_bytes=4 << 20),
        name="assemble",
    )(*pinned([table], SMEM), *parts)


def local(tokens, src_brick, merge_num, gain_attn, w_q, w_k, w_v, w_out, gain_mlp, w_in, w_back):
    frames = lax.axis_size("frame")
    spaces = lax.axis_size("space")
    _, bricks, tall, width = tokens.shape
    cap = max(2, (frames - 1) * bricks // spaces + 1)
    chunks = max(1, tall // frames // ROW_TILE)
    rows = tall // frames // chunks
    mine = lax.axis_index("frame")
    ids = jnp.stack([lax.axis_index("space"), mine]).astype(jnp.int32)
    cut = tokens.reshape(bricks, chunks * frames, rows, width)
    lay = Layout(frames, bricks, spaces, cap)
    gains = (gain_attn[None], gain_mlp[None])
    weights = (w_q, w_k, w_v, w_out, w_in, w_back)

    def across(parts, axis):
        return [exchange(part, axis, k) for k, part in enumerate(parts, 1)]

    parts = [
        [
            lax.dynamic_index_in_dim(cut, c * frames + (mine ^ k), 1, keepdims=False)
            for k in range(frames)
        ]
        for c in range(chunks)
    ]
    (src_brick, merge_num), parts = lax.optimization_barrier(((src_brick, merge_num), parts))
    arrived = [across(parts[0][1:], "frame")]
    table, *weights = prepare(lay, ids, src_brick, merge_num, weights)
    for c in range(1, chunks):
        leaving, table, arrived[-1][0] = lax.optimization_barrier(
            (parts[c][1:], table, arrived[-1][0])
        )
        arrived.append(across(leaving, "frame"))
    back = []
    for c in range(chunks):
        stacked, *slots = select(lay, table, [parts[c][0]] + arrived[c])
        pieces = [slots[0]] + across(slots[1:], "space")
        if c + 1 < chunks:
            pieces, arrived[c + 1][0] = lax.optimization_barrier((pieces, arrived[c + 1][0]))
        if c > 0:
            pieces, back[-1][3] = lax.optimization_barrier((pieces, back[-1][3]))
        done = run_block(lay, table, stacked, pieces, gains, weights)
        if c + 1 < chunks:
            arrived[c + 1], _ = lax.optimization_barrier((arrived[c + 1], done))
        returned = across(done[1:], "frame")
        back.append([done[0]] + returned)
    out = assemble(table, sum(back, []), frames)
    return out.reshape(1, bricks, tall, width)


def solution(mesh):
    tokens = P("frame", ("groups", "space"), None, None)
    tables = P(None, "groups")
    in_specs = (tokens, tables, tables) + (P(),) * 8
    return jax.shard_map(local, mesh=mesh, in_specs=in_specs, out_specs=tokens, check_vma=False)
```

```python
import functools

import jax
import jax.numpy as jnp
from jax import lax
from jax.experimental import pallas as pl
from jax.experimental.pallas import tpu as pltpu
from jax.sharding import PartitionSpec as P

HD = 64
ROW_TILE = 16
BLOCK_FF = 256
TURNED = 3

VMEM = pltpu.VMEM
SMEM = pltpu.SMEM


def spec(space):
    return pl.BlockSpec(memory_space=space)


def exchange(values, axis, step):
    size = lax.axis_size(axis)
    return lax.ppermute(values, axis, [(i, i ^ step) for i in range(size)])


def pinned(values, space):
    return [pltpu.with_memory_space_constraint(v, space) for v in values]


class Layout:
    def __init__(self, frames, bricks, spaces, cap):
        self.frames, self.bricks, self.spaces, self.cap = frames, bricks, spaces, cap
        self.requests = (frames - 1) * bricks
        self.send = 2
        self.take = self.send + spaces * cap + 1
        self.weight = self.take + self.requests
        self.size = self.weight + self.requests


def prepare_kernel(lay, ids, src, merge_num, *refs):
    held, count, sems = refs[-3:]
    half = (len(refs) - 4) // 2
    stored, table, loaded = refs[:half], refs[half], refs[half + 1 : -3]
    loads = [
        pltpu.make_async_copy(
            stored[i], held.at[i] if i < TURNED else loaded[i], sems.at[i]
        )
        for i in range(half)
    ]
    for load in loads:
        load.start()
    bricks, cap = lay.bricks, lay.cap
    me = ids[0]
    table[0] = me
    table[1] = ids[1]
    for owner in range(lay.spaces):
        count[owner] = 0

    def clear(i, carry):
        table[lay.send + i] = 0
        return carry

    lax.fori_loop(0, lay.spaces * cap + 1, clear, 0)

    def one_request(q, carry):
        frame, brick = lax.div(q, bricks), me * bricks + lax.rem(q, bricks)
        owner = lax.div(src[frame, brick], bricks)
        rank = count[owner]
        table[lay.take + q] = (owner ^ me) * cap + rank
        table[lay.weight + q] = merge_num[frame, brick]
        count[owner] = rank + 1
        return carry

    lax.fori_loop(0, lay.requests, one_request, 0)

    for i in range(TURNED):
        loads[i].wait()
        loaded[i][...] = held[i].T

    for j in range(lay.spaces):
        target = me ^ j

        def one_send(q, filled, target=target, j=j):
            frame = lax.div(q, bricks)
            source = src[frame, target * bricks + lax.rem(q, bricks)]
            owner = lax.div(source, bricks)
            table[lay.send + j * cap + filled] = frame * bricks + lax.rem(source, bricks)
            return filled + (owner == me).astype(jnp.int32)

        lax.fori_loop(0, lay.requests, one_send, 0)
    for load in loads[TURNED:]:
        load.wait()


def prepare(lay, ids, src_brick, merge_num, weights):
    return pl.pallas_call(
        functools.partial(prepare_kernel, lay),
        out_shape=(pltpu.SMEM((lay.size,), jnp.int32),)
        + tuple(pltpu.VMEM(w.shape, w.dtype) for w in weights),
        in_specs=[spec(SMEM)] * 3 + [spec(pltpu.HBM)] * len(weights),
        out_specs=(spec(SMEM),) + (spec(VMEM),) * len(weights),
        scratch_shapes=[
            VMEM((TURNED,) + weights[0].shape, weights[0].dtype),
            SMEM((lay.spaces,), jnp.int32),
            pltpu.SemaphoreType.DMA((len(weights),)),
        ],
        compiler_params=pltpu.CompilerParams(vmem_limit_bytes=6 << 20),
        name="prepare",
    )(ids, src_brick, merge_num, *pinned(weights, pltpu.HBM))


def far_first(count):
    return [*range(2, count), *range(1, min(2, count)), 0]


def select_kernel(lay, *refs):
    frames = lay.frames
    table = refs[0]
    parts = dict(zip(far_first(frames), refs[1 : 1 + frames]))
    stacked = refs[1 + frames]
    outs = refs[2 + frames :]
    mine = table[1]
    for k in range(frames):
        stacked[pl.ds((mine ^ k) * lay.bricks, lay.bricks)] = parts[k][...]
    for j in list(range(1, lay.spaces)) + [0]:
        for m in range(lay.cap):
            outs[j][m] = stacked[table[lay.send + j * lay.cap + m]]


def select(lay, table, parts):
    bricks, rows, width = parts[0].shape
    dtype = parts[0].dtype
    return pl.pallas_call(
        functools.partial(select_kernel, lay),
        out_shape=(jax.ShapeDtypeStruct((lay.frames * bricks, rows, width), dtype),)
        + (jax.ShapeDtypeStruct((lay.cap, rows, width), dtype),) * lay.spaces,
        in_specs=[spec(SMEM)] + [spec(VMEM)] * lay.frames,
        out_specs=(spec(VMEM),) * (1 + lay.spaces),
        compiler_params=pltpu.CompilerParams(vmem_limit_bytes=4 << 20),
        cost_estimate=pl.CostEstimate(flops=1, bytes_accessed=0, transcendentals=0),
        name="select",
    )(*pinned([table], SMEM), *parts)


def normalise(values, gain):
    wide = values.astype(jnp.float32)
    mean_sq = jnp.mean(wide * wide, axis=-1, keepdims=True)
    return (wide * lax.rsqrt(mean_sq + 1e-06) * gain).astype(jnp.bfloat16)


def project_turned(turned, values):
    out = lax.dot_general(
        turned, values, (((1,), (1,)), ((), ())), preferred_element_type=jnp.float32
    )
    return out.astype(jnp.bfloat16)


def gelu(x):
    scale = (2.0 / 3.141592653589793) ** 0.5
    half = 0.5 * x
    return half + half * jnp.tanh(x * (scale + (scale * 0.044715) * (x * x)))


def matmul(a, b):
    return jnp.dot(a, b, preferred_element_type=jnp.float32)


def block_kernel(lay, *refs):
    frames, bricks, cap, spaces = lay.frames, lay.bricks, lay.cap, lay.spaces
    table, stacked = refs[:2]
    pieces = refs[2 : 2 + spaces]
    gain_a, gain_m, w_q, w_k, w_v, w_o, w_in, w_back = refs[2 + spaces : 10 + spaces]
    outs = refs[10 + spaces : 10 + spaces + frames]
    slots, merged, hidden, result = refs[10 + spaces + frames :]
    rows, width = stacked.shape[1:]
    per_frame = bricks * rows
    for j in range(spaces):
        slots[j * cap : (j + 1) * cap] = pieces[j][...]
    for b in range(bricks):
        merged[b * rows : (b + 1) * rows] = stacked[b]
    for f in range(1, frames):
        for b in range(bricks):
            q = (f - 1) * bricks + b
            weight = table[lay.weight + q].astype(jnp.float32) * 0.25
            piece = slots[table[lay.take + q]].astype(jnp.float32)
            at = f * per_frame + b * rows
            merged[at : at + rows] = (
                stacked[f * bricks + b].astype(jnp.float32) + weight * piece
            ).astype(jnp.bfloat16)
    normed = normalise(merged[...], gain_a[...])
    queries = project_turned(w_q[...], normed)
    keys = project_turned(w_k[...], normed)
    vals = project_turned(w_v[...], normed)

    def heads_of(x, f):
        part = x[:, f * per_frame : (f + 1) * per_frame].astype(jnp.float32)
        return part.reshape(width // HD, HD, per_frame)

    for f in range(frames):
        query = heads_of(queries, f) * (1.0 / HD**0.5)
        scores = [
            jnp.sum(query * heads_of(keys, g), axis=1, keepdims=True) for g in range(f + 1)
        ]
        top = functools.reduce(jnp.maximum, scores)
        exps = [jnp.exp(s - top) for s in scores]
        total = functools.reduce(jnp.add, exps)
        context = None
        for g in range(f + 1):
            prob = (exps[g] / total).astype(jnp.bfloat16).astype(jnp.float32)
            term = prob * heads_of(vals, g)
            context = term if context is None else context + term
        context = context.reshape(width, per_frame).astype(jnp.bfloat16)
        hidden[f * per_frame : (f + 1) * per_frame] = context.T
    mid = (merged[...].astype(jnp.float32) + matmul(hidden[...], w_o[...])).astype(jnp.bfloat16)
    normed2 = normalise(mid, gain_m[...])
    total = mid.astype(jnp.float32)
    depth = w_in.shape[1]
    step = min(BLOCK_FF, depth)
    for at in range(0, depth, step):
        part = gelu(matmul(normed2, w_in[:, at : at + step])).astype(jnp.bfloat16)
        total = total + matmul(part, w_back[at : at + step])
    result[...] = total.astype(jnp.bfloat16).reshape(result.shape)
    mine = table[1]
    for k in range(frames):
        outs[k][...] = result[pl.ds((mine ^ k) * bricks, bricks)]


def run_block(lay, table, stacked, pieces, gains, weights):
    total, rows, width = stacked.shape
    dtype = stacked.dtype
    return pl.pallas_call(
        functools.partial(block_kernel, lay),
        out_shape=(jax.ShapeDtypeStruct((lay.bricks, rows, width), dtype),) * lay.frames,
        in_specs=[spec(SMEM)]
        + [spec(VMEM)] * (1 + lay.spaces + len(gains) + len(weights)),
        out_specs=(spec(VMEM),) * lay.frames,
        scratch_shapes=[
            VMEM((lay.spaces * lay.cap, rows, width), dtype),
            VMEM((total * rows, width), dtype),
            VMEM((total * rows, width), dtype),
            VMEM((total, rows, width), dtype),
        ],
        compiler_params=pltpu.CompilerParams(vmem_limit_bytes=20 << 20),
        cost_estimate=pl.CostEstimate(flops=10000000000, bytes_accessed=0, transcendentals=0),
        name="block",
    )(*pinned([table], SMEM), stacked, *pieces, *gains, *pinned(weights, VMEM))


def assemble_kernel(steps, chunk, *refs):
    count = len(steps)
    table = refs[0]
    parts = refs[1 : 1 + count]
    out, sems = refs[-2:]
    copies = [
        pltpu.make_async_copy(
            parts[i], out.at[:, chunk * count + (table[1] ^ k)], sems.at[i]
        )
        for i, k in enumerate(steps)
    ]
    for copy in copies:
        copy.start()
    for copy in copies:
        copy.wait()


def assemble(table, parts, steps, chunk, shape, base):
    count = len(steps)
    return pl.pallas_call(
        functools.partial(assemble_kernel, steps, chunk),
        out_shape=jax.ShapeDtypeStruct(shape, parts[0].dtype),
        in_specs=[spec(SMEM)] + [spec(VMEM)] * count + [spec(pltpu.HBM)] * len(base),
        out_specs=spec(pltpu.HBM),
        input_output_aliases={1 + count: 0} if base else {},
        scratch_shapes=[pltpu.SemaphoreType.DMA((count,))],
        compiler_params=pltpu.CompilerParams(vmem_limit_bytes=4 << 20),
        name="assemble",
    )(*pinned([table], SMEM), *parts, *base)


def local(tokens, src_brick, merge_num, gain_attn, w_q, w_k, w_v, w_out, gain_mlp, w_in, w_back):
    frames = lax.axis_size("frame")
    spaces = lax.axis_size("space")
    _, bricks, tall, width = tokens.shape
    cap = max(2, (frames - 1) * bricks // spaces + 1)
    chunks = max(1, tall // frames // ROW_TILE)
    rows = tall // frames // chunks
    mine = lax.axis_index("frame")
    ids = jnp.stack([lax.axis_index("space"), mine]).astype(jnp.int32)
    cut = tokens.reshape(bricks, chunks * frames, rows, width)
    lay = Layout(frames, bricks, spaces, cap)
    gains = (gain_attn[None], gain_mlp[None])
    weights = (w_q, w_k, w_v, w_out, w_in, w_back)

    steps = far_first(frames)

    def across(parts, axis, keys):
        return [exchange(part, axis, k) if k else part for k, part in zip(keys, parts)]

    parts = []
    for c in range(chunks):
        parts.append(
            [
                lax.dynamic_index_in_dim(cut, c * frames + (mine ^ k), 1, keepdims=False)
                for k in steps
            ]
        )
        cut, parts[c] = lax.optimization_barrier((cut, parts[c]))
    (src_brick, merge_num), parts[-1] = lax.optimization_barrier(
        ((src_brick, merge_num), parts[-1])
    )
    arrived = [across(parts[0], "frame", steps)]
    table, *weights = prepare(lay, ids, src_brick, merge_num, weights)
    for c in range(1, chunks):
        parts[c], table, arrived[-1][0] = lax.optimization_barrier(
            (parts[c], table, arrived[-1][0])
        )
        arrived.append(across(parts[c], "frame", steps))
    back = []
    stacked, *slots = select(lay, table, arrived[0])
    for c in range(chunks):
        pieces = across(slots, "space", range(spaces))
        done = run_block(lay, table, stacked, pieces, gains, weights)
        if c + 1 < chunks:
            arrived[c + 1], done = lax.optimization_barrier((arrived[c + 1], done))
            stacked, *slots = select(lay, table, arrived[c + 1])
            slots, done = lax.optimization_barrier((slots, done))
        back.append(across([done[k] for k in steps], "frame", steps))
    base = []
    for c in range(chunks):
        base = [assemble(table, back[c], steps, c, cut.shape, base)]
    [out] = base
    return out.reshape(1, bricks, tall, width)


def solution(mesh):
    tokens = P("frame", ("groups", "space"), None, None)
    tables = P(None, "groups")
    in_specs = (tokens, tables, tables) + (P(),) * 8
    return jax.shard_map(local, mesh=mesh, in_specs=in_specs, out_specs=tokens, check_vma=False)
```

```python
import functools

import jax
import jax.numpy as jnp
from jax import lax
from jax.experimental import pallas as pl
from jax.experimental.pallas import tpu as pltpu
from jax.sharding import PartitionSpec as P

HD = 64
ROW_TILE = 16
BLOCK_FF = 256
TURNED = 3

VMEM = pltpu.VMEM
SMEM = pltpu.SMEM


def spec(space):
    return pl.BlockSpec(memory_space=space)


def exchange(values, axis, step):
    size = lax.axis_size(axis)
    return lax.ppermute(values, axis, [(i, i ^ step) for i in range(size)])


def pinned(values, space):
    return [pltpu.with_memory_space_constraint(v, space) for v in values]


class Layout:
    def __init__(self, frames, bricks, spaces, cap):
        self.frames, self.bricks, self.spaces, self.cap = frames, bricks, spaces, cap
        self.requests = (frames - 1) * bricks
        self.send = 2
        self.take = self.send + spaces * cap + 1
        self.weight = self.take + self.requests
        self.size = self.weight + self.requests


def prepare_kernel(lay, ids, src, merge_num, *refs):
    held, count, sems = refs[-3:]
    half = (len(refs) - 4) // 2
    stored, table, loaded = refs[:half], refs[half], refs[half + 1 : -3]
    loads = [
        pltpu.make_async_copy(
            stored[i], held.at[i] if i < TURNED else loaded[i], sems.at[i]
        )
        for i in range(half)
    ]
    for load in loads:
        load.start()
    bricks, cap = lay.bricks, lay.cap
    me = ids[0]
    table[0] = me
    table[1] = ids[1]
    for owner in range(lay.spaces):
        count[owner] = 0

    def clear(i, carry):
        table[lay.send + i] = 0
        return carry

    lax.fori_loop(0, lay.spaces * cap + 1, clear, 0)

    def one_request(q, carry):
        frame, brick = lax.div(q, bricks), me * bricks + lax.rem(q, bricks)
        owner = lax.div(src[frame, brick], bricks)
        rank = count[owner]
        table[lay.take + q] = (owner ^ me) * cap + rank
        table[lay.weight + q] = merge_num[frame, brick]
        count[owner] = rank + 1
        return carry

    lax.fori_loop(0, lay.requests, one_request, 0)

    for i in range(TURNED):
        loads[i].wait()
        loaded[i][...] = held[i].T

    for j in range(lay.spaces):
        target = me ^ j

        def one_send(q, filled, target=target, j=j):
            frame = lax.div(q, bricks)
            source = src[frame, target * bricks + lax.rem(q, bricks)]
            owner = lax.div(source, bricks)
            table[lay.send + j * cap + filled] = frame * bricks + lax.rem(source, bricks)
            return filled + (owner == me).astype(jnp.int32)

        lax.fori_loop(0, lay.requests, one_send, 0)
    for load in loads[TURNED:]:
        load.wait()


def prepare(lay, ids, src_brick, merge_num, weights):
    return pl.pallas_call(
        functools.partial(prepare_kernel, lay),
        out_shape=(pltpu.SMEM((lay.size,), jnp.int32),)
        + tuple(pltpu.VMEM(w.shape, w.dtype) for w in weights),
        in_specs=[spec(SMEM)] * 3 + [spec(pltpu.HBM)] * len(weights),
        out_specs=(spec(SMEM),) + (spec(VMEM),) * len(weights),
        scratch_shapes=[
            VMEM((TURNED,) + weights[0].shape, weights[0].dtype),
            SMEM((lay.spaces,), jnp.int32),
            pltpu.SemaphoreType.DMA((len(weights),)),
        ],
        compiler_params=pltpu.CompilerParams(vmem_limit_bytes=6 << 20),
        name="prepare",
    )(ids, src_brick, merge_num, *pinned(weights, pltpu.HBM))


def far_first(count):
    return [*range(2, count), *range(1, min(2, count)), 0]


def select_kernel(lay, *refs):
    frames = lay.frames
    table = refs[0]
    parts = dict(zip(far_first(frames), refs[1 : 1 + frames]))
    stacked = refs[1 + frames]
    outs = refs[2 + frames :]
    mine = table[1]
    for k in range(frames):
        stacked[pl.ds((mine ^ k) * lay.bricks, lay.bricks)] = parts[k][...]
    for j in list(range(1, lay.spaces)) + [0]:
        for m in range(lay.cap):
            outs[j][m] = stacked[table[lay.send + j * lay.cap + m]]


def select(lay, table, parts):
    bricks, rows, width = parts[0].shape
    dtype = parts[0].dtype
    return pl.pallas_call(
        functools.partial(select_kernel, lay),
        out_shape=(jax.ShapeDtypeStruct((lay.frames * bricks, rows, width), dtype),)
        + (jax.ShapeDtypeStruct((lay.cap, rows, width), dtype),) * lay.spaces,
        in_specs=[spec(SMEM)] + [spec(VMEM)] * lay.frames,
        out_specs=(spec(VMEM),) * (1 + lay.spaces),
        compiler_params=pltpu.CompilerParams(vmem_limit_bytes=4 << 20),
        cost_estimate=pl.CostEstimate(flops=1, bytes_accessed=0, transcendentals=0),
        name="select",
    )(*pinned([table], SMEM), *parts)


def normalise(values, gain):
    wide = values.astype(jnp.float32)
    mean_sq = jnp.mean(wide * wide, axis=-1, keepdims=True)
    return (wide * lax.rsqrt(mean_sq + 1e-06) * gain).astype(jnp.bfloat16)


def project_turned(turned, values):
    out = lax.dot_general(
        turned, values, (((1,), (1,)), ((), ())), preferred_element_type=jnp.float32
    )
    return out.astype(jnp.bfloat16)


def gelu(x):
    scale = (2.0 / 3.141592653589793) ** 0.5
    half = 0.5 * x
    return half + half * jnp.tanh(x * (scale + (scale * 0.044715) * (x * x)))


def matmul(a, b):
    return jnp.dot(a, b, preferred_element_type=jnp.float32)


def finish(merged, context, gain, w_o, w_in, w_back):
    mid = (merged.astype(jnp.float32) + matmul(context, w_o[...])).astype(jnp.bfloat16)
    normed = normalise(mid, gain[...])
    total = mid.astype(jnp.float32)
    depth = w_in.shape[1]
    step = min(BLOCK_FF, depth)
    for at in range(0, depth, step):
        part = gelu(matmul(normed, w_in[:, at : at + step])).astype(jnp.bfloat16)
        total = total + matmul(part, w_back[at : at + step])
    return total.astype(jnp.bfloat16)


def first_kernel(lay, *refs):
    stacked, gain_a, gain_m, w_q, w_k, w_v, w_o, w_in, w_back, key, val, out = refs
    merged = stacked[: lay.bricks].reshape(-1, stacked.shape[2])
    normed = normalise(merged, gain_a[...])
    key[...] = project_turned(w_k[...], normed)
    turned = project_turned(w_v[...], normed)
    val[...] = turned
    out[...] = finish(merged, turned.T, gain_m, w_o, w_in, w_back).reshape(out.shape)


def run_first(lay, stacked, gains, weights):
    _, rows, width = stacked.shape
    dtype = stacked.dtype
    heads = jax.ShapeDtypeStruct((width, lay.bricks * rows), dtype)
    return pl.pallas_call(
        functools.partial(first_kernel, lay),
        out_shape=(heads, heads, jax.ShapeDtypeStruct((lay.bricks, rows, width), dtype)),
        in_specs=[spec(VMEM)] * (1 + len(gains) + len(weights)),
        out_specs=(spec(VMEM),) * 3,
        compiler_params=pltpu.CompilerParams(vmem_limit_bytes=12 << 20),
        cost_estimate=pl.CostEstimate(flops=10**9, bytes_accessed=0, transcendentals=0),
        name="first",
    )(stacked, *gains, *pinned(weights, VMEM))


def block_kernel(lay, *refs):
    frames, bricks, cap, spaces = lay.frames, lay.bricks, lay.cap, lay.spaces
    table, stacked, key_0, val_0, out_0 = refs[:5]
    refs = refs[5:]
    pieces = refs[:spaces]
    gain_a, gain_m, w_q, w_k, w_v, w_o, w_in, w_back = refs[spaces : 8 + spaces]
    outs = refs[8 + spaces : 8 + spaces + frames]
    slots, merged, hidden, result = refs[8 + spaces + frames :]
    rows, width = stacked.shape[1:]
    per_frame = bricks * rows
    for j in range(spaces):
        slots[j * cap : (j + 1) * cap] = pieces[j][...]
    for f in range(1, frames):
        for b in range(bricks):
            q = (f - 1) * bricks + b
            weight = table[lay.weight + q].astype(jnp.float32) * 0.25
            piece = slots[table[lay.take + q]].astype(jnp.float32)
            merged[q * rows : (q + 1) * rows] = (
                stacked[f * bricks + b].astype(jnp.float32) + weight * piece
            ).astype(jnp.bfloat16)
    normed = normalise(merged[...], gain_a[...])
    queries = project_turned(w_q[...], normed)
    keys = project_turned(w_k[...], normed)
    vals = project_turned(w_v[...], normed)

    def heads_of(x):
        return x.astype(jnp.float32).reshape(width // HD, HD, per_frame)

    def later(x, f):
        return heads_of(x[:, (f - 1) * per_frame : f * per_frame])

    key_heads = [heads_of(key_0[...])] + [later(keys, f) for f in range(1, frames)]
    val_heads = [heads_of(val_0[...])] + [later(vals, f) for f in range(1, frames)]
    for f in range(1, frames):
        query = later(queries, f) * (1.0 / HD**0.5)
        scores = [
            jnp.sum(query * key_heads[g], axis=1, keepdims=True) for g in range(f + 1)
        ]
        top = functools.reduce(jnp.maximum, scores)
        exps = [jnp.exp(s - top) for s in scores]
        total = functools.reduce(jnp.add, exps)
        context = None
        for g in range(f + 1):
            prob = (exps[g] / total).astype(jnp.bfloat16).astype(jnp.float32)
            term = prob * val_heads[g]
            context = term if context is None else context + term
        context = context.reshape(width, per_frame).astype(jnp.bfloat16)
        hidden[(f - 1) * per_frame : f * per_frame] = context.T
    done = finish(merged[...], hidden[...], gain_m, w_o, w_in, w_back)
    result[:bricks] = out_0[...]
    result[bricks:] = done.reshape(-1, rows, width)
    mine = table[1]
    for k in range(frames):
        outs[k][...] = result[pl.ds((mine ^ k) * bricks, bricks)]


def run_block(lay, table, stacked, early, pieces, gains, weights):
    total, rows, width = stacked.shape
    dtype = stacked.dtype
    return pl.pallas_call(
        functools.partial(block_kernel, lay),
        out_shape=(jax.ShapeDtypeStruct((lay.bricks, rows, width), dtype),) * lay.frames,
        in_specs=[spec(SMEM)]
        + [spec(VMEM)] * (4 + lay.spaces + len(gains) + len(weights)),
        out_specs=(spec(VMEM),) * lay.frames,
        scratch_shapes=[
            VMEM((lay.spaces * lay.cap, rows, width), dtype),
            VMEM((lay.requests * rows, width), dtype),
            VMEM((lay.requests * rows, width), dtype),
            VMEM((total, rows, width), dtype),
        ],
        compiler_params=pltpu.CompilerParams(vmem_limit_bytes=20 << 20),
        cost_estimate=pl.CostEstimate(flops=10**10, bytes_accessed=0, transcendentals=0),
        name="block",
    )(
        *pinned([table], SMEM),
        stacked,
        *early,
        *pieces,
        *gains,
        *pinned(weights, VMEM),
    )


def assemble_kernel(steps, chunk, *refs):
    count = len(steps)
    table = refs[0]
    parts = refs[1 : 1 + count]
    out, sems = refs[-2:]
    copies = [
        pltpu.make_async_copy(
            parts[i], out.at[:, chunk * count + (table[1] ^ k)], sems.at[i]
        )
        for i, k in enumerate(steps)
    ]
    for copy in copies:
        copy.start()
    for copy in copies:
        copy.wait()


def assemble(table, parts, steps, chunk, shape, base):
    count = len(steps)
    return pl.pallas_call(
        functools.partial(assemble_kernel, steps, chunk),
        out_shape=jax.ShapeDtypeStruct(shape, parts[0].dtype),
        in_specs=[spec(SMEM)] + [spec(VMEM)] * count + [spec(pltpu.HBM)] * len(base),
        out_specs=spec(pltpu.HBM),
        input_output_aliases={1 + count: 0} if base else {},
        scratch_shapes=[pltpu.SemaphoreType.DMA((count,))],
        compiler_params=pltpu.CompilerParams(vmem_limit_bytes=4 << 20),
        name="assemble",
    )(*pinned([table], SMEM), *parts, *base)


def local(tokens, src_brick, merge_num, gain_attn, w_q, w_k, w_v, w_out, gain_mlp, w_in, w_back):
    frames = lax.axis_size("frame")
    spaces = lax.axis_size("space")
    _, bricks, tall, width = tokens.shape
    cap = max(2, (frames - 1) * bricks // spaces + 1)
    chunks = max(1, tall // frames // ROW_TILE)
    rows = tall // frames // chunks
    mine = lax.axis_index("frame")
    ids = jnp.stack([lax.axis_index("space"), mine]).astype(jnp.int32)
    cut = tokens.reshape(bricks, chunks * frames, rows, width)
    lay = Layout(frames, bricks, spaces, cap)
    gains = (gain_attn[None], gain_mlp[None])
    weights = (w_q, w_k, w_v, w_out, w_in, w_back)

    steps = far_first(frames)

    def across(parts, axis, keys):
        return [exchange(part, axis, k) if k else part for k, part in zip(keys, parts)]

    parts = []
    for c in range(chunks):
        parts.append(
            [
                lax.dynamic_index_in_dim(cut, c * frames + (mine ^ k), 1, keepdims=False)
                for k in steps
            ]
        )
        cut, parts[c] = lax.optimization_barrier((cut, parts[c]))
    (src_brick, merge_num), parts[-1] = lax.optimization_barrier(
        ((src_brick, merge_num), parts[-1])
    )
    arrived = [across(parts[0], "frame", steps)]
    table, *weights = prepare(lay, ids, src_brick, merge_num, weights)
    for c in range(1, chunks):
        parts[c], table, arrived[-1][0] = lax.optimization_barrier(
            (parts[c], table, arrived[-1][0])
        )
        arrived.append(across(parts[c], "frame", steps))
    back = []
    stacked, *slots = select(lay, table, arrived[0])
    for c in range(chunks):
        pieces = across(slots, "space", range(spaces))
        if c > 0:
            pieces, back[0][1] = lax.optimization_barrier((pieces, back[0][1]))
        early = run_first(lay, stacked, gains, weights)
        done = run_block(lay, table, stacked, early, pieces, gains, weights)
        if c + 1 < chunks:
            arrived[c + 1][0], done = lax.optimization_barrier((arrived[c + 1][0], done))
            stacked, *slots = select(lay, table, arrived[c + 1])
        back.append(across([done[k] for k in steps], "frame", steps))
    base = []
    for c in range(chunks):
        base = [assemble(table, back[c], steps, c, cut.shape, base)]
    [out] = base
    return out.reshape(1, bricks, tall, width)


def solution(mesh):
    tokens = P("frame", ("groups", "space"), None, None)
    tables = P(None, "groups")
    in_specs = (tokens, tables, tables) + (P(),) * 8
    return jax.shard_map(local, mesh=mesh, in_specs=in_specs, out_specs=tokens, check_vma=False)
```

```python
import functools

import jax
import jax.numpy as jnp
from jax import lax
from jax.experimental import pallas as pl
from jax.experimental.pallas import tpu as pltpu
from jax.sharding import PartitionSpec as P

HD = 64
ROW_TILE = 16
BLOCK_FF = 256
TURNED = 3

VMEM = pltpu.VMEM
SMEM = pltpu.SMEM


def spec(space):
    return pl.BlockSpec(memory_space=space)


def exchange(values, axis, step):
    size = lax.axis_size(axis)
    return lax.ppermute(values, axis, [(i, i ^ step) for i in range(size)])


def pinned(values, space):
    return [pltpu.with_memory_space_constraint(v, space) for v in values]


class Layout:
    def __init__(self, frames, bricks, spaces, cap):
        self.frames, self.bricks, self.spaces, self.cap = frames, bricks, spaces, cap
        self.requests = (frames - 1) * bricks
        self.send = 2
        self.take = self.send + spaces * cap + 1
        self.weight = self.take + self.requests
        self.size = self.weight + self.requests


def prepare_kernel(lay, ids, src, merge_num, *refs):
    held, count, sems = refs[-3:]
    half = (len(refs) - 4) // 2
    stored, table, loaded = refs[:half], refs[half], refs[half + 1 : -3]
    loads = [
        pltpu.make_async_copy(
            stored[i], held.at[i] if i < TURNED else loaded[i], sems.at[i]
        )
        for i in range(half)
    ]
    for load in loads:
        load.start()
    bricks, cap = lay.bricks, lay.cap
    me = ids[0]
    table[0] = me
    table[1] = ids[1]
    for owner in range(lay.spaces):
        count[owner] = 0

    def clear(i, carry):
        table[lay.send + i] = 0
        return carry

    lax.fori_loop(0, lay.spaces * cap + 1, clear, 0)

    def one_request(q, carry):
        frame, brick = lax.div(q, bricks), me * bricks + lax.rem(q, bricks)
        owner = lax.div(src[frame, brick], bricks)
        rank = count[owner]
        table[lay.take + q] = (owner ^ me) * cap + rank
        table[lay.weight + q] = merge_num[frame, brick]
        count[owner] = rank + 1
        return carry

    lax.fori_loop(0, lay.requests, one_request, 0)

    for i in range(TURNED):
        loads[i].wait()
        loaded[i][...] = held[i].T

    for j in range(lay.spaces):
        target = me ^ j

        def one_send(q, filled, target=target, j=j):
            frame = lax.div(q, bricks)
            source = src[frame, target * bricks + lax.rem(q, bricks)]
            owner = lax.div(source, bricks)
            table[lay.send + j * cap + filled] = frame * bricks + lax.rem(source, bricks)
            return filled + (owner == me).astype(jnp.int32)

        lax.fori_loop(0, lay.requests, one_send, 0)
    for load in loads[TURNED:]:
        load.wait()


def prepare(lay, ids, src_brick, merge_num, weights):
    return pl.pallas_call(
        functools.partial(prepare_kernel, lay),
        out_shape=(pltpu.SMEM((lay.size,), jnp.int32),)
        + tuple(pltpu.VMEM(w.shape, w.dtype) for w in weights),
        in_specs=[spec(SMEM)] * 3 + [spec(pltpu.HBM)] * len(weights),
        out_specs=(spec(SMEM),) + (spec(VMEM),) * len(weights),
        scratch_shapes=[
            VMEM((TURNED,) + weights[0].shape, weights[0].dtype),
            SMEM((lay.spaces,), jnp.int32),
            pltpu.SemaphoreType.DMA((len(weights),)),
        ],
        compiler_params=pltpu.CompilerParams(vmem_limit_bytes=6 << 20),
        name="prepare",
    )(ids, src_brick, merge_num, *pinned(weights, pltpu.HBM))


def far_first(count):
    return [*range(2, count), *range(1, min(2, count)), 0]


def select_kernel(lay, *refs):
    frames = lay.frames
    table = refs[0]
    parts = dict(zip(far_first(frames), refs[1 : 1 + frames]))
    stacked = refs[1 + frames]
    outs = refs[2 + frames :]
    mine = table[1]
    for k in range(frames):
        stacked[pl.ds((mine ^ k) * lay.bricks, lay.bricks)] = parts[k][...]
    for j in list(range(1, lay.spaces)) + [0]:
        for m in range(lay.cap):
            outs[j][m] = stacked[table[lay.send + j * lay.cap + m]]


def select(lay, table, parts):
    bricks, rows, width = parts[0].shape
    dtype = parts[0].dtype
    return pl.pallas_call(
        functools.partial(select_kernel, lay),
        out_shape=(jax.ShapeDtypeStruct((lay.frames * bricks, rows, width), dtype),)
        + (jax.ShapeDtypeStruct((lay.cap, rows, width), dtype),) * lay.spaces,
        in_specs=[spec(SMEM)] + [spec(VMEM)] * lay.frames,
        out_specs=(spec(VMEM),) * (1 + lay.spaces),
        compiler_params=pltpu.CompilerParams(vmem_limit_bytes=4 << 20),
        cost_estimate=pl.CostEstimate(flops=1, bytes_accessed=0, transcendentals=0),
        name="select",
    )(*pinned([table], SMEM), *parts)


def normalise(values, gain):
    wide = values.astype(jnp.float32)
    mean_sq = jnp.mean(wide * wide, axis=-1, keepdims=True)
    return (wide * lax.rsqrt(mean_sq + 1e-06) * gain).astype(jnp.bfloat16)


def project_turned(turned, values):
    out = lax.dot_general(
        turned, values, (((1,), (1,)), ((), ())), preferred_element_type=jnp.float32
    )
    return out.astype(jnp.bfloat16)


def gelu(x):
    scale = (2.0 / 3.141592653589793) ** 0.5
    half = 0.5 * x
    return half + half * jnp.tanh(x * (scale + (scale * 0.044715) * (x * x)))


def matmul(a, b):
    return jnp.dot(a, b, preferred_element_type=jnp.float32)


def finish(merged, context, gain, w_o, w_in, w_back):
    mid = (merged.astype(jnp.float32) + matmul(context, w_o[...])).astype(jnp.bfloat16)
    normed = normalise(mid, gain[...])
    total = mid.astype(jnp.float32)
    depth = w_in.shape[1]
    step = min(BLOCK_FF, depth)
    for at in range(0, depth, step):
        part = gelu(matmul(normed, w_in[:, at : at + step])).astype(jnp.bfloat16)
        total = total + matmul(part, w_back[at : at + step])
    return total.astype(jnp.bfloat16)


def first_kernel(lay, *refs):
    stacked, gain_a, gain_m, w_q, w_k, w_v, w_o, w_in, w_back, key, val, out = refs
    merged = stacked[: lay.bricks].reshape(-1, stacked.shape[2])
    normed = normalise(merged, gain_a[...])
    key[...] = project_turned(w_k[...], normed)
    turned = project_turned(w_v[...], normed)
    val[...] = turned
    out[...] = finish(merged, turned.T, gain_m, w_o, w_in, w_back).reshape(out.shape)


def run_first(lay, stacked, gains, weights):
    _, rows, width = stacked.shape
    dtype = stacked.dtype
    heads = jax.ShapeDtypeStruct((width, lay.bricks * rows), dtype)
    return pl.pallas_call(
        functools.partial(first_kernel, lay),
        out_shape=(heads, heads, jax.ShapeDtypeStruct((lay.bricks, rows, width), dtype)),
        in_specs=[spec(VMEM)] * (1 + len(gains) + len(weights)),
        out_specs=(spec(VMEM),) * 3,
        compiler_params=pltpu.CompilerParams(vmem_limit_bytes=12 << 20),
        cost_estimate=pl.CostEstimate(flops=10**9, bytes_accessed=0, transcendentals=0),
        name="first",
    )(stacked, *gains, *pinned(weights, VMEM))


def block_kernel(lay, *refs):
    frames, bricks, cap, spaces = lay.frames, lay.bricks, lay.cap, lay.spaces
    table, stacked, key_0, val_0, out_0 = refs[:5]
    refs = refs[5:]
    pieces = refs[:spaces]
    gain_a, gain_m, w_q, w_k, w_v, w_o, w_in, w_back = refs[spaces : 8 + spaces]
    outs = refs[8 + spaces : 8 + spaces + frames]
    slots, merged, hidden, result = refs[8 + spaces + frames :]
    rows, width = stacked.shape[1:]
    per_frame = bricks * rows
    for j in range(spaces):
        slots[j * cap : (j + 1) * cap] = pieces[j][...]
    for f in range(1, frames):
        for b in range(bricks):
            q = (f - 1) * bricks + b
            weight = table[lay.weight + q].astype(jnp.float32) * 0.25
            piece = slots[table[lay.take + q]].astype(jnp.float32)
            merged[q * rows : (q + 1) * rows] = (
                stacked[f * bricks + b].astype(jnp.float32) + weight * piece
            ).astype(jnp.bfloat16)
    normed = normalise(merged[...], gain_a[...])
    queries = project_turned(w_q[...], normed)
    keys = project_turned(w_k[...], normed)
    vals = project_turned(w_v[...], normed)

    def heads_of(x):
        return x.astype(jnp.float32).reshape(width // HD, HD, per_frame)

    def later(x, f):
        return heads_of(x[:, (f - 1) * per_frame : f * per_frame])

    key_heads = [heads_of(key_0[...])] + [later(keys, f) for f in range(1, frames)]
    val_heads = [heads_of(val_0[...])] + [later(vals, f) for f in range(1, frames)]
    for f in range(1, frames):
        query = later(queries, f) * (1.0 / HD**0.5)
        scores = [
            jnp.sum(query * key_heads[g], axis=1, keepdims=True) for g in range(f + 1)
        ]
        top = functools.reduce(jnp.maximum, scores)
        exps = [jnp.exp(s - top) for s in scores]
        total = functools.reduce(jnp.add, exps)
        context = None
        for g in range(f + 1):
            prob = (exps[g] / total).astype(jnp.bfloat16).astype(jnp.float32)
            term = prob * val_heads[g]
            context = term if context is None else context + term
        context = context.reshape(width, per_frame).astype(jnp.bfloat16)
        hidden[(f - 1) * per_frame : f * per_frame] = context.T
    done = finish(merged[...], hidden[...], gain_m, w_o, w_in, w_back)
    result[:bricks] = out_0[...]
    result[bricks:] = done.reshape(-1, rows, width)
    mine = table[1]
    for k in range(frames):
        outs[k][...] = result[pl.ds((mine ^ k) * bricks, bricks)]


def run_block(lay, table, stacked, early, pieces, gains, weights):
    total, rows, width = stacked.shape
    dtype = stacked.dtype
    return pl.pallas_call(
        functools.partial(block_kernel, lay),
        out_shape=(jax.ShapeDtypeStruct((lay.bricks, rows, width), dtype),) * lay.frames,
        in_specs=[spec(SMEM)]
        + [spec(VMEM)] * (4 + lay.spaces + len(gains) + len(weights)),
        out_specs=(spec(VMEM),) * lay.frames,
        scratch_shapes=[
            VMEM((lay.spaces * lay.cap, rows, width), dtype),
            VMEM((lay.requests * rows, width), dtype),
            VMEM((lay.requests * rows, width), dtype),
            VMEM((total, rows, width), dtype),
        ],
        compiler_params=pltpu.CompilerParams(vmem_limit_bytes=20 << 20),
        cost_estimate=pl.CostEstimate(flops=10**10, bytes_accessed=0, transcendentals=0),
        name="block",
    )(
        *pinned([table], SMEM),
        stacked,
        *early,
        *pieces,
        *gains,
        *pinned(weights, VMEM),
    )


def assemble_kernel(steps, chunk, *refs):
    count = len(steps)
    table = refs[0]
    parts = refs[1 : 1 + count]
    out, sems = refs[-2:]
    copies = [
        pltpu.make_async_copy(
            parts[i], out.at[:, chunk * count + (table[1] ^ k)], sems.at[i]
        )
        for i, k in enumerate(steps)
    ]
    for copy in copies:
        copy.start()
    for copy in copies:
        copy.wait()


def assemble(table, parts, steps, chunk, shape, base):
    count = len(steps)
    return pl.pallas_call(
        functools.partial(assemble_kernel, steps, chunk),
        out_shape=jax.ShapeDtypeStruct(shape, parts[0].dtype),
        in_specs=[spec(SMEM)] + [spec(VMEM)] * count + [spec(pltpu.HBM)] * len(base),
        out_specs=spec(pltpu.HBM),
        input_output_aliases={1 + count: 0} if base else {},
        scratch_shapes=[pltpu.SemaphoreType.DMA((count,))],
        compiler_params=pltpu.CompilerParams(vmem_limit_bytes=4 << 20),
        name="assemble",
    )(*pinned([table], SMEM), *parts, *base)


def local(tokens, src_brick, merge_num, gain_attn, w_q, w_k, w_v, w_out, gain_mlp, w_in, w_back):
    frames = lax.axis_size("frame")
    spaces = lax.axis_size("space")
    _, bricks, tall, width = tokens.shape
    cap = max(2, (frames - 1) * bricks // spaces + 1)
    chunks = max(1, tall // frames // ROW_TILE)
    rows = tall // frames // chunks
    mine = lax.axis_index("frame")
    ids = jnp.stack([lax.axis_index("space"), mine]).astype(jnp.int32)
    cut = tokens.reshape(bricks, chunks * frames, rows, width)
    lay = Layout(frames, bricks, spaces, cap)
    gains = (gain_attn[None], gain_mlp[None])
    weights = (w_q, w_k, w_v, w_out, w_in, w_back)

    steps = far_first(frames)

    def across(parts, axis, keys):
        return [exchange(part, axis, k) if k else part for k, part in zip(keys, parts)]

    parts = []
    for c in range(chunks):
        parts.append(
            [
                lax.dynamic_index_in_dim(cut, c * frames + (mine ^ k), 1, keepdims=False)
                for k in steps
            ]
        )
        cut, parts[c] = lax.optimization_barrier((cut, parts[c]))
    (src_brick, merge_num), parts[-1] = lax.optimization_barrier(
        ((src_brick, merge_num), parts[-1])
    )
    arrived = [across(parts[0], "frame", steps)]
    table, *weights = prepare(lay, ids, src_brick, merge_num, weights)
    for c in range(1, chunks):
        parts[c], table, arrived[-1][0] = lax.optimization_barrier(
            (parts[c], table, arrived[-1][0])
        )
        arrived.append(across(parts[c], "frame", steps))
    back = []
    stacked, *slots = select(lay, table, arrived[0])
    for c in range(chunks):
        pieces = across(slots, "space", range(spaces))
        if c > 0:
            pieces, back[0][1] = lax.optimization_barrier((pieces, back[0][1]))
        if c + 1 < chunks:
            pieces, arrived[c + 1][-2] = lax.optimization_barrier((pieces, arrived[c + 1][-2]))
        early = run_first(lay, stacked, gains, weights)
        done = run_block(lay, table, stacked, early, pieces, gains, weights)
        if c + 1 < chunks:
            arrived[c + 1][0], done = lax.optimization_barrier((arrived[c + 1][0], done))
            stacked, *slots = select(lay, table, arrived[c + 1])
        back.append(across([done[k] for k in steps], "frame", steps))
    base = []
    for c in range(chunks):
        base = [assemble(table, back[c], steps, c, cut.shape, base)]
    [out] = base
    return out.reshape(1, bricks, tall, width)


def solution(mesh):
    tokens = P("frame", ("groups", "space"), None, None)
    tables = P(None, "groups")
    in_specs = (tokens, tables, tables) + (P(),) * 8
    return jax.shard_map(local, mesh=mesh, in_specs=in_specs, out_specs=tokens, check_vma=False)
```

```python
import functools

import jax
import jax.numpy as jnp
from jax import lax
from jax.experimental import pallas as pl
from jax.experimental.pallas import tpu as pltpu
from jax.sharding import PartitionSpec as P

HD = 64
ROW_TILE = 16
BLOCK_FF = 256
TURNED = 3

VMEM = pltpu.VMEM
SMEM = pltpu.SMEM


def spec(space):
    return pl.BlockSpec(memory_space=space)


def exchange(values, axis, step):
    size = lax.axis_size(axis)
    return lax.ppermute(values, axis, [(i, i ^ step) for i in range(size)])


def pinned(values, space):
    return [pltpu.with_memory_space_constraint(v, space) for v in values]


class Layout:
    def __init__(self, frames, bricks, spaces, cap):
        self.frames, self.bricks, self.spaces, self.cap = frames, bricks, spaces, cap
        self.requests = (frames - 1) * bricks
        self.send = 2
        self.take = self.send + spaces * cap + 1
        self.weight = self.take + self.requests
        self.size = self.weight + self.requests


def prepare_kernel(lay, ids, src, merge_num, *refs):
    held, count, sems = refs[-3:]
    half = (len(refs) - 4) // 2
    stored, table, loaded = refs[:half], refs[half], refs[half + 1 : -3]
    loads = [
        pltpu.make_async_copy(
            stored[i], held.at[i] if i < TURNED else loaded[i], sems.at[i]
        )
        for i in range(half)
    ]
    for load in loads:
        load.start()
    bricks, cap = lay.bricks, lay.cap
    me = ids[0]
    table[0] = me
    table[1] = ids[1]
    for owner in range(lay.spaces):
        count[owner] = 0

    def clear(i, carry):
        table[lay.send + i] = 0
        return carry

    lax.fori_loop(0, lay.spaces * cap + 1, clear, 0)

    def one_request(q, carry):
        frame, brick = lax.div(q, bricks), me * bricks + lax.rem(q, bricks)
        owner = lax.div(src[frame, brick], bricks)
        rank = count[owner]
        table[lay.take + q] = (owner ^ me) * cap + rank
        table[lay.weight + q] = merge_num[frame, brick]
        count[owner] = rank + 1
        return carry

    lax.fori_loop(0, lay.requests, one_request, 0)

    for i in range(TURNED):
        loads[i].wait()
        loaded[i][...] = held[i].T

    for j in range(lay.spaces):
        target = me ^ j

        def one_send(q, filled, target=target, j=j):
            frame = lax.div(q, bricks)
            source = src[frame, target * bricks + lax.rem(q, bricks)]
            owner = lax.div(source, bricks)
            table[lay.send + j * cap + filled] = frame * bricks + lax.rem(source, bricks)
            return filled + (owner == me).astype(jnp.int32)

        lax.fori_loop(0, lay.requests, one_send, 0)
    for load in loads[TURNED:]:
        load.wait()


def prepare(lay, ids, src_brick, merge_num, weights):
    return pl.pallas_call(
        functools.partial(prepare_kernel, lay),
        out_shape=(pltpu.SMEM((lay.size,), jnp.int32),)
        + tuple(pltpu.VMEM(w.shape, w.dtype) for w in weights),
        in_specs=[spec(SMEM)] * 3 + [spec(pltpu.HBM)] * len(weights),
        out_specs=(spec(SMEM),) + (spec(VMEM),) * len(weights),
        scratch_shapes=[
            VMEM((TURNED,) + weights[0].shape, weights[0].dtype),
            SMEM((lay.spaces,), jnp.int32),
            pltpu.SemaphoreType.DMA((len(weights),)),
        ],
        compiler_params=pltpu.CompilerParams(vmem_limit_bytes=6 << 20),
        name="prepare",
    )(ids, src_brick, merge_num, *pinned(weights, pltpu.HBM))


def far_first(count):
    return [*range(2, count), *range(1, min(2, count)), 0]


def select_kernel(lay, *refs):
    frames = lay.frames
    table = refs[0]
    parts = dict(zip(far_first(frames), refs[1 : 1 + frames]))
    stacked = refs[1 + frames]
    outs = refs[2 + frames :]
    mine = table[1]
    for k in range(frames):
        stacked[pl.ds((mine ^ k) * lay.bricks, lay.bricks)] = parts[k][...]
    for j in list(range(1, lay.spaces)) + [0]:
        for m in range(lay.cap):
            outs[j][m] = stacked[table[lay.send + j * lay.cap + m]]


def select(lay, table, parts):
    bricks, rows, width = parts[0].shape
    dtype = parts[0].dtype
    return pl.pallas_call(
        functools.partial(select_kernel, lay),
        out_shape=(jax.ShapeDtypeStruct((lay.frames * bricks, rows, width), dtype),)
        + (jax.ShapeDtypeStruct((lay.cap, rows, width), dtype),) * lay.spaces,
        in_specs=[spec(SMEM)] + [spec(VMEM)] * lay.frames,
        out_specs=(spec(VMEM),) * (1 + lay.spaces),
        compiler_params=pltpu.CompilerParams(vmem_limit_bytes=4 << 20),
        cost_estimate=pl.CostEstimate(flops=1, bytes_accessed=0, transcendentals=0),
        name="select",
    )(*pinned([table], SMEM), *parts)


def normalise(values, gain):
    wide = values.astype(jnp.float32)
    mean_sq = jnp.mean(wide * wide, axis=-1, keepdims=True)
    return (wide * lax.rsqrt(mean_sq + 1e-06) * gain).astype(jnp.bfloat16)


def project_turned(turned, values):
    out = lax.dot_general(
        turned, values, (((1,), (1,)), ((), ())), preferred_element_type=jnp.float32
    )
    return out.astype(jnp.bfloat16)


def gelu(x):
    scale = (2.0 / 3.141592653589793) ** 0.5
    half = 0.5 * x
    return half + half * jnp.tanh(x * (scale + (scale * 0.044715) * (x * x)))


def matmul(a, b):
    return jnp.dot(a, b, preferred_element_type=jnp.float32)


def finish(merged, context, gain, w_o, w_in, w_back):
    mid = (merged.astype(jnp.float32) + matmul(context, w_o[...])).astype(jnp.bfloat16)
    normed = normalise(mid, gain[...])
    total = mid.astype(jnp.float32)
    depth = w_in.shape[1]
    step = min(BLOCK_FF, depth)
    for at in range(0, depth, step):
        part = gelu(matmul(normed, w_in[:, at : at + step])).astype(jnp.bfloat16)
        total = total + matmul(part, w_back[at : at + step])
    return total.astype(jnp.bfloat16)


def first_kernel(lay, *refs):
    stacked, gain_a, gain_m, w_q, w_k, w_v, w_o, w_in, w_back, key, val, out = refs
    merged = stacked[: lay.bricks].reshape(-1, stacked.shape[2])
    normed = normalise(merged, gain_a[...])
    key[...] = project_turned(w_k[...], normed)
    turned = project_turned(w_v[...], normed)
    val[...] = turned
    out[...] = finish(merged, turned.T, gain_m, w_o, w_in, w_back).reshape(out.shape)


def run_first(lay, stacked, gains, weights):
    _, rows, width = stacked.shape
    dtype = stacked.dtype
    heads = jax.ShapeDtypeStruct((width, lay.bricks * rows), dtype)
    return pl.pallas_call(
        functools.partial(first_kernel, lay),
        out_shape=(heads, heads, jax.ShapeDtypeStruct((lay.bricks, rows, width), dtype)),
        in_specs=[spec(VMEM)] * (1 + len(gains) + len(weights)),
        out_specs=(spec(VMEM),) * 3,
        compiler_params=pltpu.CompilerParams(vmem_limit_bytes=12 << 20),
        cost_estimate=pl.CostEstimate(flops=10**9, bytes_accessed=0, transcendentals=0),
        name="first",
    )(stacked, *gains, *pinned(weights, VMEM))


def block_kernel(lay, *refs):
    frames, bricks, cap, spaces = lay.frames, lay.bricks, lay.cap, lay.spaces
    table, stacked, key_0, val_0, out_0 = refs[:5]
    refs = refs[5:]
    pieces = refs[:spaces]
    gain_a, gain_m, w_q, w_k, w_v, w_o, w_in, w_back = refs[spaces : 8 + spaces]
    outs = refs[8 + spaces : 8 + spaces + frames]
    slots, merged, hidden, result = refs[8 + spaces + frames :]
    rows, width = stacked.shape[1:]
    per_frame = bricks * rows
    for j in range(spaces):
        slots[j * cap : (j + 1) * cap] = pieces[j][...]
    for f in range(1, frames):
        for b in range(bricks):
            q = (f - 1) * bricks + b
            weight = table[lay.weight + q].astype(jnp.float32) * 0.25
            piece = slots[table[lay.take + q]].astype(jnp.float32)
            merged[q * rows : (q + 1) * rows] = (
                stacked[f * bricks + b].astype(jnp.float32) + weight * piece
            ).astype(jnp.bfloat16)
    normed = normalise(merged[...], gain_a[...])
    queries = project_turned(w_q[...], normed)
    keys = project_turned(w_k[...], normed)
    vals = project_turned(w_v[...], normed)

    def heads_of(x):
        return x.astype(jnp.float32).reshape(width // HD, HD, per_frame)

    def later(x, f):
        return heads_of(x[:, (f - 1) * per_frame : f * per_frame])

    key_heads = [heads_of(key_0[...])] + [later(keys, f) for f in range(1, frames)]
    val_heads = [heads_of(val_0[...])] + [later(vals, f) for f in range(1, frames)]
    for f in range(1, frames):
        query = later(queries, f) * (1.0 / HD**0.5)
        scores = [
            jnp.sum(query * key_heads[g], axis=1, keepdims=True) for g in range(f + 1)
        ]
        top = functools.reduce(jnp.maximum, scores)
        exps = [jnp.exp(s - top) for s in scores]
        total = functools.reduce(jnp.add, exps)
        context = None
        for g in range(f + 1):
            prob = (exps[g] / total).astype(jnp.bfloat16).astype(jnp.float32)
            term = prob * val_heads[g]
            context = term if context is None else context + term
        context = context.reshape(width, per_frame).astype(jnp.bfloat16)
        hidden[(f - 1) * per_frame : f * per_frame] = context.T
    done = finish(merged[...], hidden[...], gain_m, w_o, w_in, w_back)
    result[:bricks] = out_0[...]
    result[bricks:] = done.reshape(-1, rows, width)
    mine = table[1]
    for k in range(frames):
        outs[k][...] = result[pl.ds((mine ^ k) * bricks, bricks)]


def run_block(lay, table, stacked, early, pieces, gains, weights):
    total, rows, width = stacked.shape
    dtype = stacked.dtype
    return pl.pallas_call(
        functools.partial(block_kernel, lay),
        out_shape=(jax.ShapeDtypeStruct((lay.bricks, rows, width), dtype),) * lay.frames,
        in_specs=[spec(SMEM)]
        + [spec(VMEM)] * (4 + lay.spaces + len(gains) + len(weights)),
        out_specs=(spec(VMEM),) * lay.frames,
        scratch_shapes=[
            VMEM((lay.spaces * lay.cap, rows, width), dtype),
            VMEM((lay.requests * rows, width), dtype),
            VMEM((lay.requests * rows, width), dtype),
            VMEM((total, rows, width), dtype),
        ],
        compiler_params=pltpu.CompilerParams(vmem_limit_bytes=20 << 20),
        cost_estimate=pl.CostEstimate(flops=10**10, bytes_accessed=0, transcendentals=0),
        name="block",
    )(
        *pinned([table], SMEM),
        stacked,
        *early,
        *pieces,
        *gains,
        *pinned(weights, VMEM),
    )


def assemble_kernel(steps, chunk, *refs):
    count = len(steps)
    table = refs[0]
    parts = refs[1 : 1 + count]
    out, sems = refs[-2:]
    copies = [
        pltpu.make_async_copy(
            parts[i], out.at[:, chunk * count + (table[1] ^ k)], sems.at[i]
        )
        for i, k in enumerate(steps)
    ]
    for copy in copies:
        copy.start()
    for copy in copies:
        copy.wait()


def assemble(table, parts, steps, chunk, shape, base):
    count = len(steps)
    return pl.pallas_call(
        functools.partial(assemble_kernel, steps, chunk),
        out_shape=jax.ShapeDtypeStruct(shape, parts[0].dtype),
        in_specs=[spec(SMEM)] + [spec(VMEM)] * count + [spec(pltpu.HBM)] * len(base),
        out_specs=spec(pltpu.HBM),
        input_output_aliases={1 + count: 0} if base else {},
        scratch_shapes=[pltpu.SemaphoreType.DMA((count,))],
        compiler_params=pltpu.CompilerParams(vmem_limit_bytes=4 << 20),
        name="assemble",
    )(*pinned([table], SMEM), *parts, *base)


def local(tokens, src_brick, merge_num, gain_attn, w_q, w_k, w_v, w_out, gain_mlp, w_in, w_back):
    frames = lax.axis_size("frame")
    spaces = lax.axis_size("space")
    _, bricks, tall, width = tokens.shape
    cap = max(2, (frames - 1) * bricks // spaces + 1)
    chunks = max(1, tall // frames // ROW_TILE)
    rows = tall // frames // chunks
    mine = lax.axis_index("frame")
    ids = jnp.stack([lax.axis_index("space"), mine]).astype(jnp.int32)
    cut = tokens.reshape(bricks, chunks * frames, rows, width)
    lay = Layout(frames, bricks, spaces, cap)
    gains = (gain_attn[None], gain_mlp[None])
    weights = (w_q, w_k, w_v, w_out, w_in, w_back)

    steps = far_first(frames)

    def across(parts, axis, keys):
        return [exchange(part, axis, k) if k else part for k, part in zip(keys, parts)]

    parts = []
    for c in range(chunks):
        parts.append(
            [
                lax.dynamic_index_in_dim(cut, c * frames + (mine ^ k), 1, keepdims=False)
                for k in steps
            ]
        )
        cut, parts[c] = lax.optimization_barrier((cut, parts[c]))
    (src_brick, merge_num), parts[-1] = lax.optimization_barrier(
        ((src_brick, merge_num), parts[-1])
    )
    arrived = [across(parts[0], "frame", steps)]
    table, *weights = prepare(lay, ids, src_brick, merge_num, weights)
    for c in range(1, chunks):
        parts[c], table, arrived[-1][1] = lax.optimization_barrier(
            (parts[c], table, arrived[-1][1])
        )
        arrived.append(across(parts[c], "frame", steps))
    back = []
    stacked, *slots = select(lay, table, arrived[0])
    for c in range(chunks):
        pieces = across(slots, "space", range(spaces))
        if c > 0:
            pieces, back[0][1] = lax.optimization_barrier((pieces, back[0][1]))
        if c + 1 < chunks:
            pieces, arrived[c + 1][-2] = lax.optimization_barrier((pieces, arrived[c + 1][-2]))
        early = run_first(lay, stacked, gains, weights)
        done = run_block(lay, table, stacked, early, pieces, gains, weights)
        if c + 1 < chunks:
            arrived[c + 1][0], done = lax.optimization_barrier((arrived[c + 1][0], done))
            stacked, *slots = select(lay, table, arrived[c + 1])
        back.append(across([done[k] for k in steps], "frame", steps))
    base = []
    for c in range(chunks):
        base = [assemble(table, back[c], steps, c, cut.shape, base)]
    [out] = base
    return out.reshape(1, bricks, tall, width)


def solution(mesh):
    tokens = P("frame", ("groups", "space"), None, None)
    tables = P(None, "groups")
    in_specs = (tokens, tables, tables) + (P(),) * 8
    return jax.shard_map(local, mesh=mesh, in_specs=in_specs, out_specs=tokens, check_vma=False)
```
